128 devices in a mesh: row: 16 (over z, y), col: 8 (over x, core).
Axes of the slice: x: 4, y: 4, z: 4, core: 2. Of those that a mesh axis runs over, the one named last changes fastest.
Arguments:
- design: bfloat16 [32768, 4096], P(('row', 'col')), may hold values from -6 to 6
- weight: float32 [32768], P(('row', 'col')), may hold values from 0.2 to 5
- counts: int32 [1024], P(('row', 'col')), may hold values from 1 to 32, as said below
- column_map: int32 [4096], replicated, may hold values from 0 to 4095, each once
Outputs:
- normal: float32 [4096, 4096], P('row', 'col')
The draws below stay inside these ranges and needn't reach their ends.
Inputs may be any that keep to these rules, and one draw needn't show every extreme that they name: column_map names each of the 4096 unknowns exactly once. `counts`: an arc may hold anything from one observation to all 32 slots.
All inputs are finite; a program needn't handle non-finite values.
Results may differ from the reference program's by a relative error of at most 0.0022.
Values may be sent and summed in bfloat16 or wider, within the bound.
No kernel may reach another device: no remote copies, remote signals or barrier semaphores. Data moves between devices by JAX's collectives and lax.ppermute only.
A program may use at most 128 MiB of HBM per device.

```python
import math
import jax
import jax.numpy as jnp
from jax import lax

PANEL = 4096
ARC_ROWS = 32
ARCS_DEV = 8
ARCS = 1024
TOTAL_ROWS = 32768
N_ROW = 16
N_COL = 8


def draw_counts(key, part):
    base_key = jax.random.fold_in(key, 71)
    pick_key = jax.random.fold_in(key, 72)
    row_key = jax.random.fold_in(key, 73)
    basic = jax.random.randint(base_key, (ARCS,), 1, ARC_ROWS + 1, dtype=jnp.int32)
    full_col = jax.random.randint(pick_key, (), 0, N_COL, dtype=jnp.int32)
    full_row = jax.random.randint(row_key, (), 0, N_ROW, dtype=jnp.int32)
    arc_index = jnp.arange(ARCS, dtype=jnp.int32)
    device_of = arc_index // ARCS_DEV
    mesh_row = device_of // N_COL
    mesh_col = device_of % N_COL
    filled = jnp.logical_or(mesh_row == full_row, mesh_col == full_col)
    return jnp.where(filled, jnp.full_like(basic, ARC_ROWS), basic)


def shard_levels(own_key, shape, shards, least, top_value):
    factor_of, own = 1.0, jax.random.fold_in(own_key, 6)
    for dim, blocks in shards:
        steps = jnp.exp(jax.random.uniform(jax.random.fold_in(own, dim), (blocks,), jnp.float32, least / len(shards), top_value / len(shards)))
        factor_of = factor_of * jnp.repeat(steps, shape[dim] // blocks).reshape([-1 if axis == dim else 1 for axis in range(len(shape))])
    return factor_of


def normal_values(stream_key, shape, spread, most, split=(), held_as=jnp.bfloat16):
    result = jax.random.normal(stream_key, shape, jnp.float32) * spread
    if len(split) > 0:
        result = shard_levels(stream_key, shape, split, -0.22, 0.18) * result
    return jnp.clip(result, min=-most, max=most).astype(held_as)


def setup_inputs(seed: int = 0) -> dict:
    key_list = jax.random.split(jax.random.key(seed), 5)
    design = normal_values(key_list[0], (TOTAL_ROWS, PANEL), 1.0, 6.0, ((0, 128),))
    weight = jnp.clip(jnp.exp(math.log(5.0) - 3.218876 * jax.random.uniform(key_list[1], (TOTAL_ROWS,), jnp.float32) ** shard_levels(key_list[1], (TOTAL_ROWS,), ((0, 128),), -0.2, 0.2)), 0.2, 5.0)
    counts = draw_counts(jax.random.fold_in(key_list[4], 71), 0)
    column_map = jax.random.permutation(key_list[3], PANEL).astype(jnp.int32)
    return dict(design=design, weight=weight, counts=counts, column_map=column_map)


def reference(design, weight, counts, column_map):
    slot_index = jnp.arange(TOTAL_ROWS, dtype=jnp.int32)
    arc_of = slot_index // ARC_ROWS
    live_rows = slot_index % ARC_ROWS < counts[arc_of]
    row_scale = jnp.sqrt(jnp.where(live_rows, weight, jnp.zeros_like(weight)))
    scaled = (design.astype(jnp.float32) * row_scale[:, None]).astype(jnp.bfloat16)
    mapped = jnp.take(scaled, column_map, axis=1)
    product = lax.dot_general(mapped, mapped, (((0,), (0,)), ((), ())), preferred_element_type=jnp.float32)
    return product * (1.0 / TOTAL_ROWS)
```

```python
import functools

import jax
import jax.numpy as jnp
import numpy as np
from jax import lax
from jax.experimental import pallas as pl
from jax.experimental.pallas import tpu as pltpu
from jax.sharding import Mesh, PartitionSpec as P

ARC_ROWS = 32
AXES = ("z", "y", "x", "core")
BLK = 256
MAIN = 176
REST = BLK - MAIN
BF = jnp.bfloat16
F32 = jnp.float32


def linear(z, y, x, q):
    return ((z % 4 * 4 + y % 4) * 4 + x % 4) * 2 + q


def shift_pairs(order0, order1, sign1, stage, step):
    pairs = []
    for z in range(4):
        for y in range(4):
            for x in range(4):
                for q in range(2):
                    axis = (order0, order1)[q][stage]
                    by = step * (1, sign1)[q]
                    to = {"z": z, "y": y, "x": x}
                    to[axis] += by
                    pairs.append((linear(z, y, x, q), linear(to["z"], to["y"], to["x"], q)))
    return pairs


def mirror_pairs():
    pairs = []
    for z in range(4):
        for y in range(4):
            for x in range(4):
                for q in range(2):
                    r, c = 4 * z + y, 2 * x + q
                    i, h = r // 2, r % 2
                    if i < c:
                        to_r, to_c = 2 * c + h, i
                    elif i > c:
                        to_r, to_c = 2 * c + 1 - h, i
                    else:
                        to_r, to_c = 2 * i + 1 - h, i
                    to = linear(to_r // 4, to_r % 4, to_c // 2, to_c % 2)
                    pairs.append((linear(z, y, x, q), to))
    return pairs


MAIN_ORDER = (("x", "z", "y"), ("z", "y", "x"), 1)
REST_ORDER = (("y", "x", "z"), ("y", "x", "z"), -1)


def block_table(order, offsets, place, core):
    order0, order1, sign1 = order
    d = np.asarray(offsets, np.int32)
    at = {}
    for name in ("z", "y", "x"):
        d0 = d[:, order0.index(name)]
        d1 = d[:, order1.index(name)] * sign1
        at[name] = (place[name] + jnp.where(core == 0, d0, d1)) % 4
    r, c = 4 * at["z"] + at["y"], 2 * at["x"] + core
    i, h = r // 2, r % 2
    s = jnp.where(i <= c, h, 1 - h)
    fold = (i == c).astype(jnp.int32)
    return jnp.stack([r, 2 * c + s, 2 * c + 1 - s, fold], axis=1).reshape(-1).astype(jnp.int32)


def product_kernel(plan, table, own_ref, other_ref, *outs):
    dims = (((1,), (1,)), ((), ()))

    def dot(a, b, rows_at, rows, cols_at):
        left = a[pl.ds(rows_at, rows), :]
        right = b[pl.ds(cols_at, BLK), :]
        return lax.dot_general(left, right, dims, preferred_element_type=F32)

    for out, (first, row0, rows) in zip(outs, plan):

        @pl.loop(0, out.shape[0])
        def _(o, out=out, first=first, row0=row0, rows=rows):
            at = 4 * (first + o)
            rows_at = pl.multiple_of(table[at] * BLK + row0, 16)
            cols_at = pl.multiple_of(table[at + 1] * BLK, BLK)
            value = dot(own_ref, own_ref, rows_at, rows, cols_at)
            value += dot(other_ref, other_ref, rows_at, rows, cols_at)
            out[o] = value.astype(out.dtype)

            @pl.when(table[at + 3] == 1)
            def _():
                mixed_at = pl.multiple_of(table[at + 2] * BLK, BLK)
                mixed = dot(own_ref, own_ref, rows_at, rows, mixed_at)
                mixed += dot(other_ref, other_ref, rows_at, rows, mixed_at)
                i = lax.broadcasted_iota(jnp.int32, (rows, BLK), 0) + row0
                j = lax.broadcasted_iota(jnp.int32, (rows, BLK), 1)
                out[o] = jnp.where(i >= j, value, mixed).astype(out.dtype)


def products(own, other, parts, place, core):
    tables, plan, shapes, first = [], [], [], 0
    for order, offsets, row0, rows, kind in parts:
        tables.append(block_table(order, offsets, place, core))
        plan.append((first, row0, rows))
        shapes.append(jax.ShapeDtypeStruct((len(offsets), rows, BLK), kind))
        first += len(offsets)
    flops = sum(2 * s.shape[0] * s.shape[1] * BLK * 2 * own.shape[1] for s in shapes)
    return pl.pallas_call(
        functools.partial(product_kernel, plan),
        out_shape=shapes,
        grid_spec=pltpu.PrefetchScalarGridSpec(
            num_scalar_prefetch=1,
            grid=(1,),
            in_specs=[pl.BlockSpec(own.shape, lambda g, t: (0, 0))] * 2,
            out_specs=[pl.BlockSpec(s.shape, lambda g, t: (0, 0, 0)) for s in shapes],
        ),
        compiler_params=pltpu.CompilerParams(vmem_limit_bytes=48 * 1024 * 1024),
        cost_estimate=pl.CostEstimate(flops=flops, bytes_accessed=8 << 20, transcendentals=0),
    )(jnp.concatenate(tables), own, other)


def finish_kernel(state, scale, main_ref, rest_ref, got_ref, diag_ref, out_ref):
    s, fold = state[0], state[1] == 1
    here = jnp.concatenate([main_ref[...], rest_ref[...]], axis=0)
    got = got_ref[...].T
    mine = here.T
    i = lax.broadcasted_iota(jnp.int32, (BLK, BLK), 0)
    j = lax.broadcasted_iota(jnp.int32, (BLK, BLK), 1)
    on = jnp.logical_and(fold, i == j)
    low = jnp.logical_or(jnp.logical_not(fold), i > j)
    first = jnp.where(on, diag_ref[0:1, :], jnp.where(low, here, mine)) * scale
    second = jnp.where(on, diag_ref[1:2, :], jnp.where(low, got, here)) * scale

    @pl.when(s == 0)
    def _():
        out_ref[:, 0:BLK] = first
        out_ref[:, BLK : 2 * BLK] = second

    @pl.when(s == 1)
    def _():
        out_ref[:, BLK : 2 * BLK] = first
        out_ref[:, 0:BLK] = second


def local(design, weight, counts, column_map):
    rows_here = design.shape[0]
    core = lax.axis_index("core")
    place = {name: lax.axis_index(name) for name in ("z", "y", "x")}
    total_rows = rows_here * 128

    slot_index = jnp.arange(rows_here, dtype=jnp.int32)
    arc_of = slot_index // ARC_ROWS
    arc_table = jnp.arange(counts.shape[0], dtype=jnp.int32)
    count_of_row = jnp.sum(
        jnp.where(arc_of[:, None] == arc_table[None, :], counts[None, :], 0), axis=1
    )
    live_rows = slot_index % ARC_ROWS < count_of_row
    row_scale = jnp.sqrt(jnp.where(live_rows, weight, jnp.zeros_like(weight)))
    scaled = (design.astype(F32) * row_scale[:, None]).astype(BF)
    own = jnp.take(scaled, column_map, axis=1, mode="clip").T

    def move(array, pairs):
        return lax.ppermute(array, AXES, pairs)

    other = lax.ppermute(own, "core", [(0, 1), (1, 0)])

    wide = own.astype(F32).reshape(8, 2, BLK, rows_here)
    same = jnp.sum(wide * wide, axis=-1)
    crossed = jnp.sum(wide[:, 0] * wide[:, 1], axis=-1)
    ends = lax.psum(jnp.concatenate([same, crossed[:, None]], axis=1), AXES)

    plus = [(a, b) for a in (0, 1) for b in range(4)]
    minus = [(a, b) for a in (2, 3) for b in range(4)]
    every = plus + minus

    def offs(d, rest):
        return [(d,) + p for p in rest]

    M, R = MAIN_ORDER, REST_ORDER
    first_p, first_m, ring = products(own, other, [
        (M, offs(2, plus), 0, MAIN, BF),
        (M, offs(2, minus), 0, MAIN, BF),
        (R, offs(3, every), MAIN, REST, BF),
    ], place, core)
    side_p, side_m, ring_2 = products(own, other, [
        (M, offs(1, minus), 0, MAIN, BF),
        (M, offs(3, plus), 0, MAIN, BF),
        (R, offs(2, every), MAIN, REST, F32),
    ], place, core)
    relay_p, relay_m, ring_1, home, ring_0 = products(own, other, [
        (M, offs(1, plus), 0, MAIN, F32),
        (M, offs(3, minus), 0, MAIN, F32),
        (R, offs(1, every), MAIN, REST, F32),
        (M, offs(0, every), 0, MAIN, F32),
        (R, offs(0, every), MAIN, REST, F32),
    ], place, core)

    def main_to(stage, step):
        return shift_pairs(*M, stage, step)

    def rest_to(stage, step):
        return shift_pairs(*R, stage, step)

    got_1p = move(first_p, main_to(0, 1))
    got_1m = move(first_m, main_to(0, -1))
    got_r = move(ring, rest_to(0, 1))
    got_2p = move(side_p, main_to(0, 1))
    got_2m = move(side_m, main_to(0, -1))
    got_r = move((ring_2 + got_r.astype(F32)).astype(BF), rest_to(0, 1))
    got_3p = move((relay_p + got_1p.astype(F32)).astype(BF), main_to(0, 1))
    got_3m = move((relay_m + got_1m.astype(F32)).astype(BF), main_to(0, -1))
    got_r = move((ring_1 + got_r.astype(F32)).astype(BF), rest_to(0, 1))
    sum_p = home[:8] + got_3p.astype(F32) + got_2m.astype(F32)
    sum_m = home[8:] + got_2p.astype(F32) + got_3m.astype(F32)
    rest_sum = ring_0 + got_r.astype(F32)

    part = [sum_p[0:4], sum_p[4:8], sum_m[0:4], sum_m[4:8]]
    main_2 = part[0]
    for d in (2, 1, 3):
        main_2 = main_2 + move(part[d].astype(BF), main_to(1, d)).astype(F32)
    rest_2 = rest_sum[0:4]
    for d in (2, 1, 3):
        rest_2 = rest_2 + move(rest_sum[4 * d : 4 * d + 4].astype(BF), rest_to(1, d)).astype(F32)

    main_3 = main_2[0]
    for d in (2, 1, 3):
        main_3 = main_3 + move(main_2[d], main_to(2, d))
    rest_3 = rest_2[0]
    for d in (2, 1, 3):
        rest_3 = rest_3 + move(rest_2[d], rest_to(2, d))

    got = move(jnp.concatenate([main_3, rest_3], axis=0), mirror_pairs())

    r, c = 4 * place["z"] + place["y"], 2 * place["x"] + core
    i, h = r // 2, r % 2
    s = jnp.where(i <= c, h, 1 - h)
    state = jnp.stack([s, (i == c).astype(jnp.int32)]).astype(jnp.int32)
    picked = lax.dynamic_index_in_dim(ends, i, 0, keepdims=False)
    diag = jnp.stack([jnp.where(h == 0, picked[0], picked[1]), picked[2]])
    vmem = pl.BlockSpec(memory_space=pltpu.VMEM)
    return pl.pallas_call(
        lambda *refs: finish_kernel(refs[0], 1.0 / total_rows, *refs[1:]),
        out_shape=jax.ShapeDtypeStruct((BLK, 2 * BLK), F32),
        in_specs=[pl.BlockSpec(memory_space=pltpu.SMEM)] + [vmem] * 4,
        out_specs=vmem,
        compiler_params=pltpu.CompilerParams(vmem_limit_bytes=16 * 1024 * 1024),
    )(state, main_3, rest_3, got, diag)


def solution(mesh):
    fine = Mesh(mesh.devices.reshape(4, 4, 4, 2), AXES)
    return jax.shard_map(
        local,
        mesh=fine,
        in_specs=(P(AXES, None), P(AXES), P(AXES), P()),
        out_specs=P(("z", "y"), ("x", "core")),
        check_vma=False,
    )
```

```python
import functools

import jax
import jax.numpy as jnp
import numpy as np
from jax import lax
from jax.experimental import pallas as pl
from jax.experimental.pallas import tpu as pltpu
from jax.sharding import Mesh, PartitionSpec as P

ARC_ROWS = 32
AXES = ("z", "y", "x", "core")
BLK = 256
MAIN = 176
REST = BLK - MAIN
EXTRA = 16
BF = jnp.bfloat16
F32 = jnp.float32


def linear(z, y, x, q):
    return ((z % 4 * 4 + y % 4) * 4 + x % 4) * 2 + q


def shift_pairs(order0, order1, sign1, stage, step):
    pairs = []
    for z in range(4):
        for y in range(4):
            for x in range(4):
                for q in range(2):
                    axis = (order0, order1)[q][stage]
                    by = step * (1, sign1)[q]
                    to = {"z": z, "y": y, "x": x}
                    to[axis] += by
                    pairs.append((linear(z, y, x, q), linear(to["z"], to["y"], to["x"], q)))
    return pairs


def mirror_pairs():
    pairs = []
    for z in range(4):
        for y in range(4):
            for x in range(4):
                for q in range(2):
                    r, c = 4 * z + y, 2 * x + q
                    i, h = r // 2, r % 2
                    if i < c:
                        to_r, to_c = 2 * c + h, i
                    elif i > c:
                        to_r, to_c = 2 * c + 1 - h, i
                    else:
                        to_r, to_c = 2 * i + 1 - h, i
                    to = linear(to_r // 4, to_r % 4, to_c // 2, to_c % 2)
                    pairs.append((linear(z, y, x, q), to))
    return pairs


MAIN_ORDER = (("x", "z", "y"), ("z", "y", "x"), 1)
REST_ORDER = (("y", "x", "z"), ("y", "x", "z"), -1)


def block_table(order, offsets, place, core):
    order0, order1, sign1 = order
    d = np.asarray(offsets, np.int32)
    at = {}
    for name in ("z", "y", "x"):
        d0 = d[:, order0.index(name)]
        d1 = d[:, order1.index(name)] * sign1
        at[name] = (place[name] + jnp.where(core == 0, d0, d1)) % 4
    r, c = 4 * at["z"] + at["y"], 2 * at["x"] + core
    i, h = r // 2, r % 2
    s = jnp.where(i <= c, h, 1 - h)
    fold = (i == c).astype(jnp.int32)
    return jnp.stack([r, 2 * c + s, 2 * c + 1 - s, fold], axis=1).reshape(-1).astype(jnp.int32)


def gather_kernel(map_ref, scale_ref, design_ref, out_ref, turned, picked):
    width, half = design_ref.shape[0], design_ref.shape[0] // 2
    tiles, unroll = design_ref.shape[1] // width, 32

    @pl.loop(0, tiles)
    def _(t):
        at = pl.multiple_of(t * width, width)
        block = (design_ref[:, pl.ds(at, width)].astype(F32) * scale_ref[...]).astype(BF)
        wide = block.T.astype(F32)
        for h in range(2):
            turned[pl.ds(2 * at + h, width, 2), :] = wide[:, h * half : (h + 1) * half]

    @pl.loop(0, out_ref.shape[0] // unroll)
    def _(g):
        rows = [turned[pl.ds(2 * map_ref[g * unroll + u], 2), :] for u in range(unroll)]
        for u in range(unroll):
            picked[pl.ds(2 * (g * unroll + u), 2), :] = rows[u]

    @pl.loop(0, tiles)
    def _(t):
        at = pl.multiple_of(t * width, width)
        for h in range(2):
            out_ref[pl.ds(at, width), pl.ds(h * half, half)] = picked[
                pl.ds(2 * at + h, width, 2), :
            ].astype(BF)


def scaled_rows(column_map, row_scale, design):
    rows, unknowns = design.shape
    vmem = pl.BlockSpec(memory_space=pltpu.VMEM)
    return pl.pallas_call(
        gather_kernel,
        out_shape=jax.ShapeDtypeStruct((unknowns, rows), BF),
        in_specs=[pl.BlockSpec(memory_space=pltpu.SMEM), vmem, vmem],
        out_specs=vmem,
        scratch_shapes=[pltpu.VMEM((2 * unknowns, rows // 2), F32)] * 2,
        compiler_params=pltpu.CompilerParams(vmem_limit_bytes=20 * 1024 * 1024),
        cost_estimate=pl.CostEstimate(flops=0, bytes_accessed=16 << 20, transcendentals=0),
    )(column_map, row_scale[:, None], design)


def product_kernel(plan, turn, table, own_ref, other_ref, *refs):
    outs = refs[: len(plan)]
    both = (own_ref, other_ref)
    if turn:
        turned = refs[len(plan) :]

        @pl.loop(0, own_ref.shape[0] // BLK)
        def _(t):
            at = pl.multiple_of(t * BLK, BLK)
            for ref, to in zip(both, turned):
                to[:, pl.ds(at, BLK)] = ref[pl.ds(at, BLK), :].T

    def dot(rows_at, rows, cols_at):
        total = None
        for k, ref in enumerate(both):
            left = ref[pl.ds(rows_at, rows), :]
            if turn:
                part = jnp.dot(left, turned[k][:, pl.ds(cols_at, BLK)], preferred_element_type=F32)
            else:
                right = ref[pl.ds(cols_at, BLK), :]
                part = lax.dot_general(left, right, (((1,), (1,)), ((), ())), preferred_element_type=F32)
            total = part if total is None else total + part
        return total

    i = lax.broadcasted_iota(jnp.int32, (BLK, BLK), 0)
    j = lax.broadcasted_iota(jnp.int32, (BLK, BLK), 1)
    end = max(first + count for first, count, _, _, _ in plan)
    if any(ring for _, _, _, _, ring in plan):
        lines = []
        for e in range(4):
            at = 4 * (end + e)
            cross = dot(pl.multiple_of(table[at] * BLK, BLK), BLK, pl.multiple_of(table[at + 1] * BLK, BLK))
            lines.append(jnp.sum(jnp.where(i == j, cross, 0.0), axis=0, keepdims=True))
        lines = jnp.concatenate(lines + [jnp.zeros((EXTRA - 4, BLK), F32)], axis=0)

    for out, (first, count, row0, rows, ring) in zip(outs, plan):

        def put(o, value, out=out, rows=rows, ring=ring):
            if ring:
                out[pl.ds(pl.multiple_of(o * rows, 16), rows), :] = value.astype(out.dtype)
            else:
                out[o] = value.astype(out.dtype)

        @pl.loop(0, count // 4)
        def _(g, first=first, row0=row0, rows=rows, put=put):
            starts, values = [], []
            for u in range(4):
                at = 4 * (first + g * 4 + u)
                rows_at = pl.multiple_of(table[at] * BLK + row0, 16)
                starts.append(rows_at)
                values.append(dot(rows_at, rows, pl.multiple_of(table[at + 1] * BLK, BLK)))
            for u in range(4):
                put(g * 4 + u, values[u])
            for u in range(4):
                at = 4 * (first + g * 4 + u)

                @pl.when(table[at + 3] == 1)
                def _(u=u, at=at):
                    cols_at = pl.multiple_of(table[at + 1] * BLK, BLK)
                    mixed_at = pl.multiple_of(table[at + 2] * BLK, BLK)
                    value = dot(starts[u], rows, cols_at)
                    mixed = dot(starts[u], rows, mixed_at)
                    low = i[:rows] + row0 >= j[:rows]
                    put(g * 4 + u, jnp.where(low, value, mixed))

        if ring:
            out[pl.ds(count * rows, EXTRA), :] = lines.astype(out.dtype)


def products(own, other, parts, place, core, turn):
    tables, plan, shapes, first, flops = [], [], [], 0, 0
    for order, offsets, row0, rows, kind, ring in parts:
        count = len(offsets)
        tables.append(block_table(order, offsets, place, core))
        plan.append((first, count, row0, rows, ring))
        shape = (count * rows + EXTRA, BLK) if ring else (count, rows, BLK)
        shapes.append(jax.ShapeDtypeStruct(shape, kind))
        first += count
        flops += 4 * count * rows * BLK * own.shape[1]
    step = jnp.where(core == 0, 1, REST_ORDER[2]) * jnp.arange(4, dtype=jnp.int32)
    pair = 2 * (2 * ((place["x"] + step) % 4) + core)
    none = jnp.zeros_like(pair)
    tables.append(jnp.stack([pair, pair + 1, none, none], axis=1).reshape(-1).astype(jnp.int32))
    scratch = [pltpu.VMEM(own.shape[::-1], BF)] * 2 if turn else []
    vmem = pl.BlockSpec(memory_space=pltpu.VMEM)
    return pl.pallas_call(
        functools.partial(product_kernel, plan, turn),
        out_shape=shapes,
        in_specs=[pl.BlockSpec(memory_space=pltpu.SMEM), vmem, vmem],
        out_specs=[vmem] * len(shapes),
        scratch_shapes=scratch,
        compiler_params=pltpu.CompilerParams(vmem_limit_bytes=28 * 1024 * 1024),
        cost_estimate=pl.CostEstimate(flops=flops, bytes_accessed=8 << 20, transcendentals=0),
    )(jnp.concatenate(tables), own, other)


def finish_kernel(state, scale, main_ref, rest_ref, got_ref, cross_ref, out_ref):
    s, fold = state[0], state[1] == 1
    here = jnp.concatenate([main_ref[...], rest_ref[...]], axis=0)
    got = got_ref[...].T
    mine = here.T
    i = lax.broadcasted_iota(jnp.int32, (BLK, BLK), 0)
    j = lax.broadcasted_iota(jnp.int32, (BLK, BLK), 1)
    on = jnp.logical_and(fold, i == j)
    low = jnp.logical_or(jnp.logical_not(fold), i >= j)
    first = jnp.where(low, here, mine) * scale
    second = jnp.where(on, cross_ref[0:1, :], jnp.where(low, got, here)) * scale

    @pl.when(s == 0)
    def _():
        out_ref[:, 0:BLK] = first
        out_ref[:, BLK : 2 * BLK] = second

    @pl.when(s == 1)
    def _():
        out_ref[:, BLK : 2 * BLK] = first
        out_ref[:, 0:BLK] = second


def local(design, weight, counts, column_map):
    rows_here = design.shape[0]
    core = lax.axis_index("core")
    place = {name: lax.axis_index(name) for name in ("z", "y", "x")}
    total_rows = rows_here * 128

    slot_index = jnp.arange(rows_here, dtype=jnp.int32)
    arc_of = slot_index // ARC_ROWS
    arc_table = jnp.arange(counts.shape[0], dtype=jnp.int32)
    count_of_row = jnp.sum(
        jnp.where(arc_of[:, None] == arc_table[None, :], counts[None, :], 0), axis=1
    )
    live_rows = slot_index % ARC_ROWS < count_of_row
    row_scale = jnp.sqrt(jnp.where(live_rows, weight, jnp.zeros_like(weight)))
    own = scaled_rows(column_map, row_scale, design)

    def move(array, pairs):
        return lax.ppermute(array, AXES, pairs)

    other = lax.ppermute(own, "core", [(0, 1), (1, 0)])

    plus = [(a, b) for a in (0, 1) for b in range(4)]
    minus = [(a, b) for a in (2, 3) for b in range(4)]
    every = plus + minus

    def offs(d, rest):
        return [(d,) + p for p in rest]

    M, R = MAIN_ORDER, REST_ORDER
    first_p, first_m, ring = products(own, other, [
        (M, offs(2, plus), 0, MAIN, BF, False),
        (M, offs(2, minus), 0, MAIN, BF, False),
        (R, offs(3, every), MAIN, REST, BF, True),
    ], place, core, False)
    side_p, side_m, ring_2 = products(own, other, [
        (M, offs(1, minus), 0, MAIN, BF, False),
        (M, offs(3, plus), 0, MAIN, BF, False),
        (R, offs(2, every), MAIN, REST, F32, True),
    ], place, core, True)
    relay_p, relay_m, ring_1, home, ring_0 = products(own, other, [
        (M, offs(1, plus), 0, MAIN, F32, False),
        (M, offs(3, minus), 0, MAIN, F32, False),
        (R, offs(1, every), MAIN, REST, F32, True),
        (M, offs(0, every), 0, MAIN, F32, False),
        (R, offs(0, every), MAIN, REST, F32, True),
    ], place, core, True)

    def main_to(stage, step):
        return shift_pairs(*M, stage, step)

    def rest_to(stage, step):
        return shift_pairs(*R, stage, step)

    got_1p = move(first_p, main_to(0, 1))
    got_1m = move(first_m, main_to(0, -1))
    got_r = move(ring, rest_to(0, 1))
    got_2p = move(side_p, main_to(0, 1))
    got_2m = move(side_m, main_to(0, -1))
    got_r = move((ring_2 + got_r.astype(F32)).astype(BF), rest_to(0, 1))
    got_3p = move((relay_p + got_1p.astype(F32)).astype(BF), main_to(0, 1))
    got_3m = move((relay_m + got_1m.astype(F32)).astype(BF), main_to(0, -1))
    got_r = move((ring_1 + got_r.astype(F32)).astype(BF), rest_to(0, 1))
    sum_p = home[:8] + got_3p.astype(F32) + got_2m.astype(F32)
    sum_m = home[8:] + got_2p.astype(F32) + got_3m.astype(F32)
    rest_sum = ring_0 + got_r.astype(F32)

    part = [sum_p[0:4], sum_p[4:8], sum_m[0:4], sum_m[4:8]]
    main_2 = part[0]
    for d in (2, 1, 3):
        main_2 = main_2 + move(part[d].astype(BF), main_to(1, d)).astype(F32)
    quarter = 4 * REST
    rest_2, cross = rest_sum[:quarter], rest_sum[4 * quarter : 4 * quarter + 1]
    tail = rest_sum[4 * quarter :]
    for d in (2, 1, 3):
        piece = jnp.concatenate([rest_sum[d * quarter : (d + 1) * quarter], tail], axis=0)
        piece = move(piece.astype(BF), rest_to(1, d)).astype(F32)
        rest_2 = rest_2 + piece[:quarter]
        cross = cross + piece[quarter + d : quarter + d + 1]

    main_3 = main_2[0]
    for d in (2, 1, 3):
        main_3 = main_3 + move(main_2[d], main_to(2, d))
    rest_3, extra = rest_2[:REST], jnp.broadcast_to(cross, (8, BLK))
    cross = extra
    for d in (2, 1, 3):
        piece = jnp.concatenate([rest_2[d * REST : (d + 1) * REST], extra], axis=0)
        piece = move(piece, rest_to(2, d))
        rest_3 = rest_3 + piece[:REST]
        cross = cross + piece[REST:]

    got = move(jnp.concatenate([main_3, rest_3], axis=0), mirror_pairs())

    r, c = 4 * place["z"] + place["y"], 2 * place["x"] + core
    i, h = r // 2, r % 2
    s = jnp.where(i <= c, h, 1 - h)
    state = jnp.stack([s, (i == c).astype(jnp.int32)]).astype(jnp.int32)
    vmem = pl.BlockSpec(memory_space=pltpu.VMEM)
    return pl.pallas_call(
        lambda *refs: finish_kernel(refs[0], 1.0 / total_rows, *refs[1:]),
        out_shape=jax.ShapeDtypeStruct((BLK, 2 * BLK), F32),
        in_specs=[pl.BlockSpec(memory_space=pltpu.SMEM)] + [vmem] * 4,
        out_specs=vmem,
        compiler_params=pltpu.CompilerParams(vmem_limit_bytes=16 * 1024 * 1024),
    )(state, main_3, rest_3, got, cross)


def solution(mesh):
    fine = Mesh(mesh.devices.reshape(4, 4, 4, 2), AXES)
    return jax.shard_map(
        local,
        mesh=fine,
        in_specs=(P(AXES, None), P(AXES), P(AXES), P()),
        out_specs=P(("z", "y"), ("x", "core")),
        check_vma=False,
    )
```

```python
import functools

import jax
import jax.numpy as jnp
import numpy as np
from jax import lax
from jax.experimental import pallas as pl
from jax.experimental.pallas import tpu as pltpu
from jax.sharding import Mesh, PartitionSpec as P

ARC_ROWS = 32
AXES = ("z", "y", "x", "core")
BLK = 256
MAIN = 176
REST = BLK - MAIN
EXTRA = 16
BF = jnp.bfloat16
F32 = jnp.float32


def linear(z, y, x, q):
    return ((z % 4 * 4 + y % 4) * 4 + x % 4) * 2 + q


def shift_pairs(order0, order1, sign1, stage, step):
    pairs = []
    for z in range(4):
        for y in range(4):
            for x in range(4):
                for q in range(2):
                    axis = (order0, order1)[q][stage]
                    by = step * (1, sign1)[q]
                    to = {"z": z, "y": y, "x": x}
                    to[axis] += by
                    pairs.append((linear(z, y, x, q), linear(to["z"], to["y"], to["x"], q)))
    return pairs


def mirror_pairs():
    pairs = []
    for z in range(4):
        for y in range(4):
            for x in range(4):
                for q in range(2):
                    r, c = 4 * z + y, 2 * x + q
                    i, h = r // 2, r % 2
                    if i < c:
                        to_r, to_c = 2 * c + h, i
                    elif i > c:
                        to_r, to_c = 2 * c + 1 - h, i
                    else:
                        to_r, to_c = 2 * i + 1 - h, i
                    to = linear(to_r // 4, to_r % 4, to_c // 2, to_c % 2)
                    pairs.append((linear(z, y, x, q), to))
    return pairs


MAIN_ORDER = (("x", "z", "y"), ("z", "y", "x"), 1)
REST_ORDER = (("y", "x", "z"), ("y", "x", "z"), -1)


def block_table(order, offsets):
    order0, order1, sign1 = order
    rows = []
    for device in range(128):
        place = {"z": device // 32, "y": device // 8 % 4, "x": device // 2 % 4}
        core = device % 2
        for d in offsets:
            at = dict(place)
            for name, by in zip((order0, order1)[core], d):
                at[name] = (place[name] + by * (1, sign1)[core]) % 4
            r, c = 4 * at["z"] + at["y"], 2 * at["x"] + core
            i, h = r // 2, r % 2
            s = h if i <= c else 1 - h
            rows += [r, 2 * c + s, 2 * c + 1 - s, int(i == c)]
    return np.asarray(rows, np.int32).reshape(128, -1)


def cross_table():
    rows = []
    for device in range(128):
        x, core = device // 2 % 4, device % 2
        for d in range(4):
            first = 2 * (2 * ((x + d * (1, REST_ORDER[2])[core]) % 4) + core)
            rows += [first, first + 1, 0, 0]
    return np.asarray(rows, np.int32).reshape(128, -1)


def gather_kernel(map_ref, counts_ref, weight_ref, design_ref, out_ref, held, turned, picked, sems):
    width, half = held.shape[0], held.shape[0] // 2
    tiles, unroll, loads = held.shape[1] // width, 32, sems.shape[0]
    copies = []
    for n in range(loads):
        part = pl.ds(n * (held.shape[1] // loads), held.shape[1] // loads)
        copies.append(pltpu.make_async_copy(design_ref.at[:, part], held.at[:, part], sems.at[n]))
        copies[-1].start()

    slot = lax.broadcasted_iota(jnp.int32, (1, width), 1)
    count = jnp.zeros((1, width), jnp.int32)
    for arc in range(width // ARC_ROWS):
        count = jnp.where(slot // ARC_ROWS == arc, counts_ref[arc], count)
    weight = weight_ref[...]
    scale = jnp.sqrt(jnp.where(slot % ARC_ROWS < count, weight, jnp.zeros_like(weight)))

    for n in range(loads):
        copies[n].wait()

        @pl.loop(n * (tiles // loads), (n + 1) * (tiles // loads))
        def _(t):
            at = pl.multiple_of(t * width, width)
            wide = (held[:, pl.ds(at, width)].T.astype(F32) * scale).astype(BF).astype(F32)
            for h in range(2):
                turned[pl.ds(2 * at + h, width, 2), :] = wide[:, h * half : (h + 1) * half]

    @pl.loop(0, out_ref.shape[0] // unroll)
    def _(g):
        rows = [turned[pl.ds(2 * map_ref[g * unroll + u], 2), :] for u in range(unroll)]
        for u in range(unroll):
            picked[pl.ds(2 * (g * unroll + u), 2), :] = rows[u]

    @pl.loop(0, tiles)
    def _(t):
        at = pl.multiple_of(t * width, width)
        for h in range(2):
            out_ref[pl.ds(at, width), pl.ds(h * half, half)] = picked[
                pl.ds(2 * at + h, width, 2), :
            ].astype(BF)


def scaled_rows(column_map, counts, weight, design):
    rows, unknowns = design.shape
    vmem, smem = pl.BlockSpec(memory_space=pltpu.VMEM), pl.BlockSpec(memory_space=pltpu.SMEM)
    return pl.pallas_call(
        gather_kernel,
        out_shape=jax.ShapeDtypeStruct((unknowns, rows), BF),
        in_specs=[smem, smem, vmem, pl.BlockSpec(memory_space=pl.ANY)],
        out_specs=vmem,
        scratch_shapes=[
            pltpu.VMEM((rows, unknowns), BF),
            pltpu.VMEM((2 * unknowns, rows // 2), F32),
            pltpu.VMEM((2 * unknowns, rows // 2), F32),
            pltpu.SemaphoreType.DMA((4,)),
        ],
        compiler_params=pltpu.CompilerParams(vmem_limit_bytes=60 * 1024 * 1024),
        cost_estimate=pl.CostEstimate(flops=0, bytes_accessed=16 << 20, transcendentals=0),
    )(column_map, counts, weight[None, :], design)


def turn_kernel(rows_ref, out_ref):
    @pl.loop(0, rows_ref.shape[0] // BLK)
    def _(t):
        at = pl.multiple_of(t * BLK, BLK)
        out_ref[:, pl.ds(at, BLK)] = rows_ref[pl.ds(at, BLK), :].T


def turned_rows(rows):
    vmem = pl.BlockSpec(memory_space=pltpu.VMEM)
    return pl.pallas_call(
        turn_kernel,
        out_shape=jax.ShapeDtypeStruct(rows.shape[::-1], rows.dtype),
        in_specs=[vmem],
        out_specs=vmem,
        compiler_params=pltpu.CompilerParams(vmem_limit_bytes=12 * 1024 * 1024),
        cost_estimate=pl.CostEstimate(flops=0, bytes_accessed=4 << 20, transcendentals=0),
    )(rows)


def product_kernel(plan, table, *refs):
    if len(refs) > 2 + len(plan):
        own_ref, other_ref, own_turned_ref, *outs, held, turned, sems = refs
        deep = own_ref.shape[1]
        copies = [
            pltpu.make_async_copy(other_ref, held.at[:, pl.ds(deep, deep)], sems.at[0]),
            pltpu.make_async_copy(own_ref, held.at[:, pl.ds(0, deep)], sems.at[1]),
            pltpu.make_async_copy(own_turned_ref, turned.at[pl.ds(0, deep), :], sems.at[2]),
        ]
        for copy in copies:
            copy.start()
        copies[0].wait()

        @pl.loop(0, held.shape[0] // BLK)
        def _(t):
            at = pl.multiple_of(t * BLK, BLK)
            turned[pl.ds(deep, deep), pl.ds(at, BLK)] = held[pl.ds(at, BLK), pl.ds(deep, deep)].T

        copies[1].wait()
        copies[2].wait()
    else:
        held, turned, *outs = refs

    def dot(rows_at, rows, cols_at):
        return jnp.dot(
            held[pl.ds(rows_at, rows), :], turned[:, pl.ds(cols_at, BLK)], preferred_element_type=F32
        )

    i = lax.broadcasted_iota(jnp.int32, (BLK, BLK), 0)
    j = lax.broadcasted_iota(jnp.int32, (BLK, BLK), 1)
    if any(ring for _, _, _, _, ring in plan):
        lines = []
        for e in range(4):
            at = 4 * e
            cross = dot(pl.multiple_of(table[at] * BLK, BLK), BLK, pl.multiple_of(table[at + 1] * BLK, BLK))
            lines.append(jnp.sum(jnp.where(i == j, cross, 0.0), axis=0, keepdims=True))
        lines = jnp.concatenate(lines + [jnp.zeros((EXTRA - 4, BLK), F32)], axis=0)

    for out, (first, count, row0, rows, ring) in zip(outs, plan):

        def put(o, value, out=out, rows=rows, ring=ring):
            if ring:
                out[pl.ds(pl.multiple_of(o * rows, 16), rows), :] = value.astype(out.dtype)
            else:
                out[o] = value.astype(out.dtype)

        batch = 8 if count % 8 == 0 else 4

        @pl.loop(0, count // batch)
        def _(g, batch=batch, first=first, row0=row0, rows=rows, put=put, out=out):
            starts, values = [], []
            for u in range(batch):
                at = 4 * (first + g * batch + u)
                rows_at = pl.multiple_of(table[at] * BLK + row0, 16)
                starts.append(rows_at)
                value = dot(rows_at, rows, pl.multiple_of(table[at + 1] * BLK, BLK))
                values.append(value.astype(out.dtype))
            for u in range(batch):
                put(g * batch + u, values[u])
            for u in range(batch):
                at = 4 * (first + g * batch + u)

                @pl.when(table[at + 3] == 1)
                def _(u=u, at=at):
                    cols_at = pl.multiple_of(table[at + 1] * BLK, BLK)
                    mixed_at = pl.multiple_of(table[at + 2] * BLK, BLK)
                    value = dot(starts[u], rows, cols_at)
                    mixed = dot(starts[u], rows, mixed_at)
                    low = i[:rows] + row0 >= j[:rows]
                    put(g * batch + u, jnp.where(low, value, mixed))

        if ring:
            out[pl.ds(count * rows, EXTRA), :] = lines.astype(out.dtype)


def products(operands, parts, tables, plan, grant):
    shapes = []
    for offsets, rows, kind, ring in parts:
        count = len(offsets)
        shape = (count * rows + EXTRA, BLK) if ring else (count, rows, BLK)
        shapes.append(jax.ShapeDtypeStruct(shape, kind))
    vmem, whole = pl.BlockSpec(memory_space=pltpu.VMEM), pl.BlockSpec(memory_space=pl.ANY)
    opening = len(operands) == 3
    if opening:
        unknowns, deep = operands[0].shape
        shapes += [jax.ShapeDtypeStruct((unknowns, 2 * deep), BF), jax.ShapeDtypeStruct((2 * deep, unknowns), BF)]
    return pl.pallas_call(
        functools.partial(product_kernel, plan),
        out_shape=shapes,
        in_specs=[pl.BlockSpec(memory_space=pltpu.SMEM)] + ([vmem, whole, vmem] if opening else [vmem] * 2),
        out_specs=[vmem] * len(shapes),
        scratch_shapes=[pltpu.SemaphoreType.DMA((3,))] if opening else [],
        compiler_params=pltpu.CompilerParams(vmem_limit_bytes=grant * 1024 * 1024),
        cost_estimate=pl.CostEstimate(flops=0, bytes_accessed=1 << 20, transcendentals=0),
    )(tables, *operands)


def finish_kernel(state, scale, main_ref, rest_ref, got_main_ref, got_rest_ref, cross_ref, out_ref):
    s, fold = state[0], state[1] == 1
    here = jnp.concatenate([main_ref[...], rest_ref[...]], axis=0)
    got = jnp.concatenate([got_main_ref[...].astype(F32), got_rest_ref[...].astype(F32)], axis=0).T
    mine = here.T
    i = lax.broadcasted_iota(jnp.int32, (BLK, BLK), 0)
    j = lax.broadcasted_iota(jnp.int32, (BLK, BLK), 1)
    on = jnp.logical_and(fold, i == j)
    low = jnp.logical_or(jnp.logical_not(fold), i >= j)
    first = jnp.where(low, here, mine) * scale
    second = jnp.where(on, cross_ref[0:1, :], jnp.where(low, got, here)) * scale

    @pl.when(s == 0)
    def _():
        out_ref[:, 0:BLK] = first
        out_ref[:, BLK : 2 * BLK] = second

    @pl.when(s == 1)
    def _():
        out_ref[:, BLK : 2 * BLK] = first
        out_ref[:, 0:BLK] = second


def local(design, weight, counts, column_map):
    rows_here = design.shape[0]
    core = lax.axis_index("core")
    place = {name: lax.axis_index(name) for name in ("z", "y", "x")}
    total_rows = rows_here * 128

    own = scaled_rows(column_map, counts, weight, design)

    def move(array, pairs):
        return lax.ppermute(array, AXES, pairs)

    other = lax.ppermute(own, "core", [(0, 1), (1, 0)])

    plus = [(a, b) for a in (0, 1) for b in range(4)]
    minus = [(a, b) for a in (2, 3) for b in range(4)]
    every = plus + minus

    def offs(d, rest):
        return [(d,) + p for p in rest]

    M, R = MAIN_ORDER, REST_ORDER
    calls = [
        [(M, offs(2, plus), BF), (M, offs(2, minus), BF), (R, offs(3, every), BF)],
        [(M, offs(1, minus), BF), (M, offs(3, plus), BF), (R, offs(2, every), F32)],
        [(M, offs(1, plus), F32), (M, offs(3, minus), F32), (R, offs(1, every), F32)]
        + [(M, offs(0, every[4 * d : 4 * d + 4]), F32) for d in range(4)]
        + [(R, offs(0, every), F32)],
    ]
    tables, first, made = [cross_table()], 4, []
    device = ((place["z"] * 4 + place["y"]) * 4 + place["x"]) * 2 + core
    plans = []
    for call in calls:
        plan = []
        for order, offsets, _ in call:
            tables.append(block_table(order, offsets))
            row0, rows = (0, MAIN) if order is M else (MAIN, REST)
            plan.append((first, len(offsets), row0, rows, order is R))
            first += len(offsets)
        plans.append(plan)
    table = lax.dynamic_index_in_dim(
        jnp.asarray(np.concatenate(tables, axis=1)), device, 0, keepdims=False
    )
    operands = (own, other, turned_rows(own))
    for call, plan, grant in zip(calls, plans, (18, 18, 24)):
        parts = [(offsets, rows, kind, ring) for (_, offsets, kind), (_, _, _, rows, ring) in zip(call, plan)]
        got = products(operands, parts, table, plan, grant)
        if len(operands) == 3:
            operands = got[len(parts) :]
        made.append(got[: len(parts)])
        if len(made) == 2:
            operands, made[1] = lax.optimization_barrier((operands, made[1]))
    first_p, first_m, ring = made[0]
    side_p, side_m, ring_2 = made[1]
    relay_p, relay_m, ring_1, *home, ring_0 = made[2]

    def main_to(stage, step):
        return shift_pairs(*M, stage, step)

    def rest_to(stage, step):
        return shift_pairs(*R, stage, step)

    got_1p = move(first_p, main_to(0, 1))
    got_1m = move(first_m, main_to(0, -1))
    got_r = move(ring, rest_to(0, 1))
    got_2p = move(side_p, main_to(0, 1))
    got_2m = move(side_m, main_to(0, -1))
    got_r = move((ring_2 + got_r.astype(F32)).astype(BF), rest_to(0, 1))
    got_3p = move((relay_p + got_1p.astype(F32)).astype(BF), main_to(0, 1))
    got_3m = move((relay_m + got_1m.astype(F32)).astype(BF), main_to(0, -1))
    got_r = move((ring_1 + got_r.astype(F32)).astype(BF), rest_to(0, 1))
    part = []
    for d in range(4):
        pair = (got_3p, got_2m) if d < 2 else (got_2p, got_3m)
        half = slice(4 * (d % 2), 4 * (d % 2) + 4)
        part.append(home[d] + pair[0][half].astype(F32) + pair[1][half].astype(F32))
    rest_sum = ring_0 + got_r.astype(F32)

    main_2 = part[0]
    for d in (2, 1, 3):
        main_2 = main_2 + move(part[d].astype(BF), main_to(1, d)).astype(F32)
    quarter = 4 * REST
    rest_2, cross = rest_sum[:quarter], rest_sum[4 * quarter : 4 * quarter + 1]
    tail = rest_sum[4 * quarter :]
    for d in (2, 1, 3):
        piece = jnp.concatenate([rest_sum[d * quarter : (d + 1) * quarter], tail], axis=0)
        piece = move(piece.astype(BF), rest_to(1, d)).astype(F32)
        rest_2 = rest_2 + piece[:quarter]
        cross = cross + piece[quarter + d : quarter + d + 1]

    main_3 = main_2[0]
    for d in (2, 1, 3):
        main_3 = main_3 + move(main_2[d], main_to(2, d))
    rest_3, extra = rest_2[:REST], jnp.broadcast_to(cross, (8, BLK))
    cross = extra
    for d in (2, 1, 3):
        piece = jnp.concatenate([rest_2[d * REST : (d + 1) * REST], extra], axis=0)
        piece = move(piece, rest_to(2, d))
        rest_3 = rest_3 + piece[:REST]
        cross = cross + piece[REST:]

    got_main = move(main_3.astype(BF), mirror_pairs())
    got_rest = move(rest_3.astype(BF), mirror_pairs())

    r, c = 4 * place["z"] + place["y"], 2 * place["x"] + core
    i, h = r // 2, r % 2
    s = jnp.where(i <= c, h, 1 - h)
    state = jnp.stack([s, (i == c).astype(jnp.int32)]).astype(jnp.int32)
    vmem = pl.BlockSpec(memory_space=pltpu.VMEM)
    return pl.pallas_call(
        lambda *refs: finish_kernel(refs[0], 1.0 / total_rows, *refs[1:]),
        out_shape=jax.ShapeDtypeStruct((BLK, 2 * BLK), F32),
        in_specs=[pl.BlockSpec(memory_space=pltpu.SMEM)] + [vmem] * 5,
        out_specs=vmem,
        compiler_params=pltpu.CompilerParams(vmem_limit_bytes=16 * 1024 * 1024),
    )(state, main_3, rest_3, got_main, got_rest, cross)


def solution(mesh):
    fine = Mesh(mesh.devices.reshape(4, 4, 4, 2), AXES)
    return jax.shard_map(
        local,
        mesh=fine,
        in_specs=(P(AXES, None), P(AXES), P(AXES), P()),
        out_specs=P(("z", "y"), ("x", "core")),
        check_vma=False,
    )
```

```python
import functools

import jax
import jax.numpy as jnp
import numpy as np
from jax import lax
from jax.experimental import pallas as pl
from jax.experimental.pallas import tpu as pltpu
from jax.sharding import Mesh, PartitionSpec as P

ARC_ROWS = 32
AXES = ("z", "y", "x", "core")
BLK = 256
MAIN = 176
REST = BLK - MAIN
GRANT_FIRST = 24
EXTRA = 16
BF = jnp.bfloat16
F32 = jnp.float32


def linear(z, y, x, q):
    return ((z % 4 * 4 + y % 4) * 4 + x % 4) * 2 + q


def shift_pairs(order0, order1, sign1, stage, step):
    pairs = []
    for z in range(4):
        for y in range(4):
            for x in range(4):
                for q in range(2):
                    axis = (order0, order1)[q][stage]
                    by = step * (1, sign1)[q]
                    to = {"z": z, "y": y, "x": x}
                    to[axis] += by
                    pairs.append((linear(z, y, x, q), linear(to["z"], to["y"], to["x"], q)))
    return pairs


def mirror_pairs():
    pairs = []
    for z in range(4):
        for y in range(4):
            for x in range(4):
                for q in range(2):
                    r, c = 4 * z + y, 2 * x + q
                    i, h = r // 2, r % 2
                    if i < c:
                        to_r, to_c = 2 * c + h, i
                    elif i > c:
                        to_r, to_c = 2 * c + 1 - h, i
                    else:
                        to_r, to_c = 2 * i + 1 - h, i
                    to = linear(to_r // 4, to_r % 4, to_c // 2, to_c % 2)
                    pairs.append((linear(z, y, x, q), to))
    return pairs


MAIN_ORDER = (("x", "z", "y"), ("z", "y", "x"), 1)
REST_ORDER = (("y", "x", "z"), ("y", "x", "z"), -1)


def block_table(order, offsets):
    order0, order1, sign1 = order
    rows = []
    for device in range(128):
        place = {"z": device // 32, "y": device // 8 % 4, "x": device // 2 % 4}
        core = device % 2
        for d in offsets:
            at = dict(place)
            for name, by in zip((order0, order1)[core], d):
                at[name] = (place[name] + by * (1, sign1)[core]) % 4
            r, c = 4 * at["z"] + at["y"], 2 * at["x"] + core
            i, h = r // 2, r % 2
            s = h if i <= c else 1 - h
            rows += [r, 2 * c + s, 2 * c + 1 - s, int(i == c)]
    return np.asarray(rows, np.int32).reshape(128, -1)


def cross_table():
    rows = []
    for device in range(128):
        x, core = device // 2 % 4, device % 2
        for d in range(4):
            first = 2 * (2 * ((x + d * (1, REST_ORDER[2])[core]) % 4) + core)
            rows += [first, first + 1, 0, 0]
    return np.asarray(rows, np.int32).reshape(128, -1)


def pick_rows(map_ref, first, columns, picked, out_ref):
    width, half, unroll = out_ref.shape[1], out_ref.shape[1] // 2, 32

    @pl.loop(0, out_ref.shape[0] // unroll)
    def _(g):
        rows = [columns[pl.ds(2 * map_ref[first + g * unroll + u], 2), :] for u in range(unroll)]
        for u in range(unroll):
            picked[pl.ds(2 * (g * unroll + u), 2), :] = rows[u]

    @pl.loop(0, out_ref.shape[0] // width)
    def _(t):
        at = pl.multiple_of(t * width, width)
        for h in range(2):
            out_ref[pl.ds(at, width), pl.ds(h * half, half)] = picked[
                pl.ds(2 * at + h, width, 2), :
            ].astype(BF)


def first_pick_kernel(map_ref, counts_ref, weight_ref, design_ref, columns, out_ref, held, picked, sems):
    width, half = held.shape[0], held.shape[0] // 2
    tiles, loads = held.shape[1] // width, sems.shape[0]
    copies = []
    for n in range(loads):
        part = pl.ds(n * (held.shape[1] // loads), held.shape[1] // loads)
        copies.append(pltpu.make_async_copy(design_ref.at[:, part], held.at[:, part], sems.at[n]))
        copies[-1].start()

    slot = lax.broadcasted_iota(jnp.int32, (1, width), 1)
    count = jnp.zeros((1, width), jnp.int32)
    for arc in range(width // ARC_ROWS):
        count = jnp.where(slot // ARC_ROWS == arc, counts_ref[arc], count)
    weight = weight_ref[...]
    scale = jnp.sqrt(jnp.where(slot % ARC_ROWS < count, weight, jnp.zeros_like(weight)))

    for n in range(loads):
        copies[n].wait()

        @pl.loop(n * (tiles // loads), (n + 1) * (tiles // loads))
        def _(t):
            at = pl.multiple_of(t * width, width)
            wide = (held[:, pl.ds(at, width)].T.astype(F32) * scale).astype(BF).astype(F32)
            for h in range(2):
                columns[pl.ds(2 * at + h, width, 2), :] = wide[:, h * half : (h + 1) * half]

    pick_rows(map_ref, 0, columns, picked, out_ref)


def second_pick_kernel(map_ref, columns, out_ref, picked):
    pick_rows(map_ref, out_ref.shape[0], columns, picked, out_ref)


def cost(size):
    return pl.CostEstimate(flops=0, bytes_accessed=size << 20, transcendentals=0)


def grant(size):
    return pltpu.CompilerParams(vmem_limit_bytes=size * 1024 * 1024)


def scaled_rows(column_map, counts, weight, design):
    rows, unknowns = design.shape
    vmem, smem = pl.BlockSpec(memory_space=pltpu.VMEM), pl.BlockSpec(memory_space=pltpu.SMEM)
    part = jax.ShapeDtypeStruct((unknowns // 2, rows), BF)
    picked = pltpu.VMEM((unknowns, rows // 2), F32)
    columns, low = pl.pallas_call(
        first_pick_kernel,
        out_shape=[jax.ShapeDtypeStruct((2 * unknowns, rows // 2), F32), part],
        in_specs=[smem, smem, vmem, pl.BlockSpec(memory_space=pl.ANY)],
        out_specs=[vmem, vmem],
        scratch_shapes=[pltpu.VMEM((rows, unknowns), BF), picked, pltpu.SemaphoreType.DMA((4,))],
        compiler_params=grant(GRANT_FIRST),
        cost_estimate=cost(8),
    )(column_map, counts, weight[None, :], design)
    high = pl.pallas_call(
        second_pick_kernel,
        out_shape=part,
        in_specs=[smem, vmem],
        out_specs=vmem,
        scratch_shapes=[picked],
        compiler_params=grant(16),
        cost_estimate=cost(8),
    )(column_map, columns)
    return low, high


def turn(from_ref, to_ref, row, column):
    deep = from_ref.shape[1]

    @pl.loop(0, from_ref.shape[0] // BLK)
    def _(t):
        at = pl.multiple_of(t * BLK, BLK)
        to_ref[pl.ds(row, deep), pl.ds(column + at, BLK)] = from_ref[pl.ds(at, BLK), :].T


def turn_kernel(own_low, own_high, other_low, own_out, low_out):
    turn(own_low, own_out, 0, 0)
    turn(own_high, own_out, 0, own_low.shape[0])
    turn(other_low, low_out, 0, 0)


def product_kernel(plan, opening, cross_made, cross_used, table, *refs):
    if opening:
        own_low, own_high, other_low, other_high, own_turned, low_turned, *outs, sems = refs
        *outs, held, turned = outs
        terms, lines = [], None
        half, deep = own_low.shape
        pieces = [
            (own_low, held.at[pl.ds(0, half), pl.ds(0, deep)]),
            (own_high, held.at[pl.ds(half, half), pl.ds(0, deep)]),
            (other_low, held.at[pl.ds(0, half), pl.ds(deep, deep)]),
            (other_high, held.at[pl.ds(half, half), pl.ds(deep, deep)]),
            (own_turned, turned.at[pl.ds(0, deep), :]),
            (low_turned, turned.at[pl.ds(deep, deep), pl.ds(0, half)]),
        ]
        copies = [pltpu.make_async_copy(a, b, sems.at[n]) for n, (a, b) in enumerate(pieces)]
        for copy in copies:
            copy.start()
        turn(other_high, turned, deep, half)
        for copy in copies:
            copy.wait()
    else:
        held, turned, *outs = refs
        lines = None
        if cross_used:
            lines, *outs = outs
            lines = lines[...]
        count = len(outs) - len(plan) - int(cross_made)
        terms, outs = outs[:count], outs[count:]

    def dot(rows_at, rows, cols_at):
        return jnp.dot(
            held[pl.ds(rows_at, rows), :], turned[:, pl.ds(cols_at, BLK)], preferred_element_type=F32
        )

    i = lax.broadcasted_iota(jnp.int32, (BLK, BLK), 0)
    j = lax.broadcasted_iota(jnp.int32, (BLK, BLK), 1)
    if cross_made:
        *outs, cross_out = outs
        made = []
        for e in range(4):
            at = 4 * e
            cross = dot(pl.multiple_of(table[at] * BLK, BLK), BLK, pl.multiple_of(table[at + 1] * BLK, BLK))
            made.append(jnp.sum(jnp.where(i == j, cross, 0.0), axis=0, keepdims=True))
        lines = jnp.concatenate(made + [jnp.zeros((EXTRA - 4, BLK), F32)], axis=0)
        cross_out[...] = lines

    for out, (first, count, row0, rows, ring, added) in zip(outs, plan):

        def plus(o, value, rows=rows, ring=ring, added=added):
            for n, at in added:
                if ring:
                    term = terms[n][pl.ds(pl.multiple_of((at + o) * rows, 16), rows), :]
                else:
                    term = terms[n][at + o]
                value = value + term.astype(F32)
            return value

        def put(o, value, out=out, rows=rows, ring=ring):
            if ring:
                out[pl.ds(pl.multiple_of(o * rows, 16), rows), :] = value
            else:
                out[o] = value

        batch = 8 if count % 8 == 0 else 4

        @pl.loop(0, count // batch)
        def _(g, batch=batch, first=first, row0=row0, rows=rows, put=put, plus=plus, out=out):
            starts, values = [], []
            for u in range(batch):
                at = 4 * (first + g * batch + u)
                rows_at = pl.multiple_of(table[at] * BLK + row0, 16)
                starts.append(rows_at)
                value = dot(rows_at, rows, pl.multiple_of(table[at + 1] * BLK, BLK))
                values.append(plus(g * batch + u, value).astype(out.dtype))
            for u in range(batch):
                put(g * batch + u, values[u])
            for u in range(batch):
                at = 4 * (first + g * batch + u)

                @pl.when(table[at + 3] == 1)
                def _(u=u, at=at):
                    cols_at = pl.multiple_of(table[at + 1] * BLK, BLK)
                    mixed_at = pl.multiple_of(table[at + 2] * BLK, BLK)
                    value = dot(starts[u], rows, cols_at)
                    mixed = dot(starts[u], rows, mixed_at)
                    low = i[:rows] + row0 >= j[:rows]
                    value = plus(g * batch + u, jnp.where(low, value, mixed))
                    put(g * batch + u, value.astype(out.dtype))

        if ring:
            total = lines
            for n, _ in added:
                total = total + terms[n][pl.ds(16 * REST, EXTRA), :].astype(F32)
            out[pl.ds(count * rows, EXTRA), :] = total.astype(out.dtype)


def products(operands, table, plan, kinds, cross=None, cross_made=False, terms=(), weight=1):
    shapes = []
    for (_, count, _, rows, ring, _), kind in zip(plan, kinds):
        shape = (count * rows + EXTRA, BLK) if ring else (count, rows, BLK)
        shapes.append(jax.ShapeDtypeStruct(shape, kind))
    if cross_made:
        shapes.append(jax.ShapeDtypeStruct((EXTRA, BLK), F32))
    vmem = pl.BlockSpec(memory_space=pltpu.VMEM)
    opening = len(operands) == 6
    if opening:
        half, deep = operands[0].shape
        shapes += [jax.ShapeDtypeStruct((2 * half, 2 * deep), BF), jax.ShapeDtypeStruct((2 * deep, 2 * half), BF)]
    extra = () if cross is None else (cross,)
    return pl.pallas_call(
        functools.partial(product_kernel, plan, opening, cross_made, cross is not None),
        out_shape=shapes,
        in_specs=[pl.BlockSpec(memory_space=pltpu.SMEM)] + [vmem] * (len(operands) + len(extra) + len(terms)),
        out_specs=[vmem] * len(shapes),
        scratch_shapes=[pltpu.SemaphoreType.DMA((6,))] if opening else [],
        compiler_params=grant(24),
        cost_estimate=cost(weight),
    )(table, *operands, *extra, *terms)


def call_sum(kernel, shapes, *operands):
    vmem = pl.BlockSpec(memory_space=pltpu.VMEM)
    return pl.pallas_call(
        kernel,
        out_shape=[jax.ShapeDtypeStruct(shape, kind) for shape, kind in shapes],
        in_specs=[vmem] * len(operands),
        out_specs=[vmem] * len(shapes),
        compiler_params=grant(12),
        cost_estimate=cost(1),
    )(*operands)


def main_sum_kernel(own, second, first, third, *outs):
    for d, out in enumerate(outs):
        total = own[d]
        for ref in (second, first, third):
            total = total + ref[d].astype(F32)
        out[...] = total


def rest_sum_kernel(own, second, first, third, *outs):
    quarter = own.shape[0] - EXTRA
    cross = own[pl.ds(quarter, EXTRA), :][0:1]
    for d, ref in ((2, second), (1, first), (3, third)):
        cross = cross + ref[pl.ds(quarter, EXTRA), :].astype(F32)[d : d + 1]
    cross = jnp.broadcast_to(cross, (8, BLK))
    for d, out in enumerate(outs):
        part = pl.ds(d * REST, REST)
        total = own[part, :]
        for ref in (second, first, third):
            total = total + ref[part, :].astype(F32)
        out[pl.ds(0, REST), :] = total
        out[pl.ds(REST, 8), :] = cross


def last_sum_kernel(own, second, first, third, out, sent):
    total = own[...] + second[...] + first[...] + third[...]
    out[...] = total
    sent[...] = total[: sent.shape[0]].astype(sent.dtype)


def finish_kernel(state, scale, main_ref, rest_ref, got_main_ref, got_rest_ref, out_ref):
    s, fold = state[0], state[1] == 1
    here = jnp.concatenate([main_ref[...], rest_ref[0:REST, :]], axis=0)
    got = jnp.concatenate([got_main_ref[...].astype(F32), got_rest_ref[...].astype(F32)], axis=0).T
    mine = here.T
    i = lax.broadcasted_iota(jnp.int32, (BLK, BLK), 0)
    j = lax.broadcasted_iota(jnp.int32, (BLK, BLK), 1)
    on = jnp.logical_and(fold, i == j)
    low = jnp.logical_or(jnp.logical_not(fold), i >= j)
    first = jnp.where(low, here, mine) * scale
    second = jnp.where(on, rest_ref[REST : REST + 1, :], jnp.where(low, got, here)) * scale

    @pl.when(s == 0)
    def _():
        out_ref[:, 0:BLK] = first
        out_ref[:, BLK : 2 * BLK] = second

    @pl.when(s == 1)
    def _():
        out_ref[:, BLK : 2 * BLK] = first
        out_ref[:, 0:BLK] = second


def local(design, weight, counts, column_map):
    rows_here = design.shape[0]
    core = lax.axis_index("core")
    place = {name: lax.axis_index(name) for name in ("z", "y", "x")}
    total_rows = rows_here * 128

    own_low, own_high = scaled_rows(column_map, counts, weight, design)

    def move(array, pairs):
        return lax.ppermute(array, AXES, pairs)

    M, R = MAIN_ORDER, REST_ORDER

    def main_to(stage, step):
        return shift_pairs(*M, stage, step)

    def rest_to(stage, step):
        return shift_pairs(*R, stage, step)

    swap = [(0, 1), (1, 0)]
    other_low = lax.ppermute(own_low, "core", swap)
    other_high = lax.ppermute(own_high, "core", swap)
    half = own_low.shape
    own_turned, low_turned = pl.pallas_call(
        turn_kernel,
        out_shape=[
            jax.ShapeDtypeStruct((half[1], 2 * half[0]), BF),
            jax.ShapeDtypeStruct((half[1], half[0]), BF),
        ],
        in_specs=[pl.BlockSpec(memory_space=pltpu.VMEM)] * 3,
        out_specs=[pl.BlockSpec(memory_space=pltpu.VMEM)] * 2,
        compiler_params=grant(12),
        cost_estimate=cost(1),
    )(own_low, own_high, other_low)

    plus = [(a, b) for a in (0, 1) for b in range(4)]
    minus = [(a, b) for a in (2, 3) for b in range(4)]
    every = plus + minus
    tables = [cross_table()]

    def blocks(order, d, rest, *added):
        first = sum(t.shape[1] for t in tables) // 4
        tables.append(block_table(order, [(d,) + p for p in rest]))
        row0, rows = (0, MAIN) if order is M else (MAIN, REST)
        return first, len(rest), row0, rows, order is R, added

    plan_1 = [blocks(M, 2, plus), blocks(M, 2, minus)]
    plan_1r = [blocks(R, 3, every)]
    plan_2 = [blocks(M, 1, minus), blocks(M, 3, plus)]
    plan_2r = [blocks(R, 2, every, (0, 0))]
    plan_3 = [blocks(M, 1, plus, (0, 0)), blocks(M, 3, minus, (1, 0))]
    plan_3r = [blocks(R, 1, every, (0, 0))]
    plan_4 = [
        blocks(M, 0, every[4 * d : 4 * d + 4], (2 * (d // 2), 4 * (d % 2)), (2 * (d // 2) + 1, 4 * (d % 2)))
        for d in range(4)
    ]
    plan_4r = [blocks(R, 0, every[4 * d : 4 * d + 4], (0, 4 * d)) for d in range(4)]
    device = ((place["z"] * 4 + place["y"]) * 4 + place["x"]) * 2 + core
    table = lax.dynamic_index_in_dim(
        jnp.asarray(np.concatenate(tables, axis=1)), device, 0, keepdims=False
    )

    pieces = (own_low, own_high, other_low, other_high, own_turned, low_turned)
    ring, cross, *both = products(pieces, table, plan_1r, (BF,), cross_made=True)
    got_r = move(ring, rest_to(0, 1))
    first_p, first_m = products(both, table, plan_1, (BF, BF))
    got_1p = move(first_p, main_to(0, 1))
    got_1m = move(first_m, main_to(0, -1))
    both, first_p = lax.optimization_barrier((both, first_p))
    side_p, side_m = products(both, table, plan_2, (BF, BF))
    got_2p = move(side_p, main_to(0, 1))
    got_2m = move(side_m, main_to(0, -1))
    both, side_p = lax.optimization_barrier((both, side_p))
    (ring,) = products(both, table, plan_2r, (BF,), cross, terms=(got_r,))
    got_r = move(ring, rest_to(0, 1))
    both, ring = lax.optimization_barrier((both, ring))
    relay_p, relay_m = products(both, table, plan_3, (BF, BF), terms=(got_1p, got_1m))
    got_3p = move(relay_p, main_to(0, 1))
    got_3m = move(relay_m, main_to(0, -1))
    both, relay_p, got_2p, got_2m = lax.optimization_barrier((both, relay_p, got_2p, got_2m))
    (ring,) = products(both, table, plan_3r, (BF,), cross, terms=(got_r,), weight=60)
    got_r = move(ring, rest_to(0, 1))
    both, ring = lax.optimization_barrier((both, ring))
    part = products(both, table, plan_4, (F32, BF, BF, BF), terms=(got_3p, got_2m, got_2p, got_3m))
    rest = products(both, table, plan_4r, (F32, BF, BF, BF), cross, terms=(got_r,))

    got = [move(part[d], main_to(1, d)) for d in (2, 1, 3)]
    got_r = [move(rest[d], rest_to(1, d)) for d in (2, 1, 3)]
    part = call_sum(main_sum_kernel, [((MAIN, BLK), F32)] * 4, part[0], *got)
    rest = call_sum(rest_sum_kernel, [((REST + 8, BLK), F32)] * 4, rest[0], *got_r)

    got = [move(part[d], main_to(2, d)) for d in (2, 1, 3)]
    got_r = [move(rest[d], rest_to(2, d)) for d in (2, 1, 3)]
    main_3, main_sent = call_sum(last_sum_kernel, [((MAIN, BLK), F32), ((MAIN, BLK), BF)], part[0], *got)
    rest_3, rest_sent = call_sum(last_sum_kernel, [((REST + 8, BLK), F32), ((REST, BLK), BF)], rest[0], *got_r)
    got_main = move(main_sent, mirror_pairs())
    got_rest = move(rest_sent, mirror_pairs())

    r, c = 4 * place["z"] + place["y"], 2 * place["x"] + core
    i, h = r // 2, r % 2
    s = jnp.where(i <= c, h, 1 - h)
    state = jnp.stack([s, (i == c).astype(jnp.int32)]).astype(jnp.int32)
    vmem = pl.BlockSpec(memory_space=pltpu.VMEM)
    return pl.pallas_call(
        lambda *refs: finish_kernel(refs[0], 1.0 / total_rows, *refs[1:]),
        out_shape=jax.ShapeDtypeStruct((BLK, 2 * BLK), F32),
        in_specs=[pl.BlockSpec(memory_space=pltpu.SMEM)] + [vmem] * 4,
        out_specs=vmem,
        compiler_params=pltpu.CompilerParams(vmem_limit_bytes=16 * 1024 * 1024),
    )(state, main_3, rest_3, got_main, got_rest)


def solution(mesh):
    fine = Mesh(mesh.devices.reshape(4, 4, 4, 2), AXES)
    return jax.shard_map(
        local,
        mesh=fine,
        in_specs=(P(AXES, None), P(AXES), P(AXES), P()),
        out_specs=P(("z", "y"), ("x", "core")),
        check_vma=False,
    )
```

```python
import functools

import jax
import jax.numpy as jnp
import numpy as np
from jax import lax
from jax.experimental import pallas as pl
from jax.experimental.pallas import tpu as pltpu
from jax.sharding import Mesh, PartitionSpec as P

ARC_ROWS = 32
AXES = ("z", "y", "x", "core")
BLK = 256
MAIN = 176
REST = BLK - MAIN
GRANT_FIRST = 24
WEIGHT = 20
EXTRA = 16
BF = jnp.bfloat16
F32 = jnp.float32


def linear(z, y, x, q):
    return ((z % 4 * 4 + y % 4) * 4 + x % 4) * 2 + q


def shift_pairs(order0, order1, sign1, stage, step):
    pairs = []
    for z in range(4):
        for y in range(4):
            for x in range(4):
                for q in range(2):
                    axis = (order0, order1)[q][stage]
                    by = step * (1, sign1)[q]
                    to = {"z": z, "y": y, "x": x}
                    to[axis] += by
                    pairs.append((linear(z, y, x, q), linear(to["z"], to["y"], to["x"], q)))
    return pairs


def mirror_pairs():
    pairs = []
    for z in range(4):
        for y in range(4):
            for x in range(4):
                for q in range(2):
                    r, c = 4 * z + y, 2 * x + q
                    i, h = r // 2, r % 2
                    if i < c:
                        to_r, to_c = 2 * c + h, i
                    elif i > c:
                        to_r, to_c = 2 * c + 1 - h, i
                    else:
                        to_r, to_c = 2 * i + 1 - h, i
                    to = linear(to_r // 4, to_r % 4, to_c // 2, to_c % 2)
                    pairs.append((linear(z, y, x, q), to))
    return pairs


MAIN_ORDER = (("x", "z", "y"), ("z", "y", "x"), 1)
REST_ORDER = (("y", "x", "z"), ("y", "x", "z"), -1)


def block_table(order, offsets):
    order0, order1, sign1 = order
    rows = []
    for device in range(128):
        place = {"z": device // 32, "y": device // 8 % 4, "x": device // 2 % 4}
        core = device % 2
        for d in offsets:
            at = dict(place)
            for name, by in zip((order0, order1)[core], d):
                at[name] = (place[name] + by * (1, sign1)[core]) % 4
            r, c = 4 * at["z"] + at["y"], 2 * at["x"] + core
            i, h = r // 2, r % 2
            s = h if i <= c else 1 - h
            rows += [r, 2 * c + s, 2 * c + 1 - s, int(i == c)]
    return np.asarray(rows, np.int32).reshape(128, -1)


def cross_table():
    rows = []
    for device in range(128):
        x, core = device // 2 % 4, device % 2
        for d in range(4):
            first = 2 * (2 * ((x + d * (1, REST_ORDER[2])[core]) % 4) + core)
            rows += [first, first + 1, 0, 0]
    return np.asarray(rows, np.int32).reshape(128, -1)


def pick_rows(map_ref, first, columns, picked, out_ref):
    width, half, unroll = out_ref.shape[1], out_ref.shape[1] // 2, 32

    @pl.loop(0, out_ref.shape[0] // unroll)
    def _(g):
        rows = [columns[pl.ds(2 * map_ref[first + g * unroll + u], 2), :] for u in range(unroll)]
        for u in range(unroll):
            picked[pl.ds(2 * (g * unroll + u), 2), :] = rows[u]

    @pl.loop(0, out_ref.shape[0] // width)
    def _(t):
        at = pl.multiple_of(t * width, width)
        for h in range(2):
            out_ref[pl.ds(at, width), pl.ds(h * half, half)] = picked[
                pl.ds(2 * at + h, width, 2), :
            ].astype(BF)


def first_pick_kernel(map_ref, counts_ref, weight_ref, design_ref, columns, out_ref, held, picked, sems):
    width, half = held.shape[0], held.shape[0] // 2
    tiles, loads = held.shape[1] // width, sems.shape[0]
    copies = []
    for n in range(loads):
        part = pl.ds(n * (held.shape[1] // loads), held.shape[1] // loads)
        copies.append(pltpu.make_async_copy(design_ref.at[:, part], held.at[:, part], sems.at[n]))
        copies[-1].start()

    slot = lax.broadcasted_iota(jnp.int32, (1, width), 1)
    count = jnp.zeros((1, width), jnp.int32)
    for arc in range(width // ARC_ROWS):
        count = jnp.where(slot // ARC_ROWS == arc, counts_ref[arc], count)
    weight = weight_ref[...]
    scale = jnp.sqrt(jnp.where(slot % ARC_ROWS < count, weight, jnp.zeros_like(weight)))

    for n in range(loads):
        copies[n].wait()

        @pl.loop(n * (tiles // loads), (n + 1) * (tiles // loads))
        def _(t):
            at = pl.multiple_of(t * width, width)
            wide = (held[:, pl.ds(at, width)].T.astype(F32) * scale).astype(BF).astype(F32)
            for h in range(2):
                columns[pl.ds(2 * at + h, width, 2), :] = wide[:, h * half : (h + 1) * half]

    pick_rows(map_ref, 0, columns, picked, out_ref)


def second_pick_kernel(map_ref, columns, out_ref, picked):
    pick_rows(map_ref, out_ref.shape[0], columns, picked, out_ref)


def cost(size):
    return pl.CostEstimate(flops=0, bytes_accessed=size << 20, transcendentals=0)


def grant(size):
    return pltpu.CompilerParams(vmem_limit_bytes=size * 1024 * 1024)


def scaled_rows(column_map, counts, weight, design):
    rows, unknowns = design.shape
    vmem, smem = pl.BlockSpec(memory_space=pltpu.VMEM), pl.BlockSpec(memory_space=pltpu.SMEM)
    part = jax.ShapeDtypeStruct((unknowns // 2, rows), BF)
    picked = pltpu.VMEM((unknowns, rows // 2), F32)
    columns, low = pl.pallas_call(
        first_pick_kernel,
        out_shape=[jax.ShapeDtypeStruct((2 * unknowns, rows // 2), F32), part],
        in_specs=[smem, smem, vmem, pl.BlockSpec(memory_space=pl.ANY)],
        out_specs=[vmem, vmem],
        scratch_shapes=[pltpu.VMEM((rows, unknowns), BF), picked, pltpu.SemaphoreType.DMA((4,))],
        compiler_params=grant(GRANT_FIRST),
        cost_estimate=cost(8),
    )(column_map, counts, weight[None, :], design)
    high = pl.pallas_call(
        second_pick_kernel,
        out_shape=part,
        in_specs=[smem, vmem],
        out_specs=vmem,
        scratch_shapes=[picked],
        compiler_params=grant(16),
        cost_estimate=cost(8),
    )(column_map, columns)
    return low, high


def turn(from_ref, to_ref, row, column):
    deep = from_ref.shape[1]

    @pl.loop(0, from_ref.shape[0] // BLK)
    def _(t):
        at = pl.multiple_of(t * BLK, BLK)
        to_ref[pl.ds(row, deep), pl.ds(column + at, BLK)] = from_ref[pl.ds(at, BLK), :].T


def turn_kernel(own_low, own_high, other_low, own_out, low_out):
    turn(own_low, own_out, 0, 0)
    turn(own_high, own_out, 0, own_low.shape[0])
    turn(other_low, low_out, 0, 0)


def product_kernel(plan, opening, cross_made, cross_used, table, *refs):
    if opening:
        own_low, own_high, other_low, other_high, own_turned, low_turned, *outs, sems = refs
        *outs, held, turned = outs
        terms, lines = [], None
        half, deep = own_low.shape
        pieces = [
            (own_low, held.at[pl.ds(0, half), pl.ds(0, deep)]),
            (own_high, held.at[pl.ds(half, half), pl.ds(0, deep)]),
            (other_low, held.at[pl.ds(0, half), pl.ds(deep, deep)]),
            (other_high, held.at[pl.ds(half, half), pl.ds(deep, deep)]),
            (own_turned, turned.at[pl.ds(0, deep), :]),
            (low_turned, turned.at[pl.ds(deep, deep), pl.ds(0, half)]),
        ]
        copies = [pltpu.make_async_copy(a, b, sems.at[n]) for n, (a, b) in enumerate(pieces)]
        for copy in copies:
            copy.start()
        turn(other_high, turned, deep, half)
        for copy in copies:
            copy.wait()
    else:
        held, turned, *outs = refs
        lines = None
        if cross_used:
            lines, *outs = outs
            lines = lines[...]
        count = len(outs) - len(plan) - int(cross_made)
        terms, outs = outs[:count], outs[count:]

    def dot(rows_at, rows, cols_at):
        return jnp.dot(
            held[pl.ds(rows_at, rows), :], turned[:, pl.ds(cols_at, BLK)], preferred_element_type=F32
        )

    i = lax.broadcasted_iota(jnp.int32, (BLK, BLK), 0)
    j = lax.broadcasted_iota(jnp.int32, (BLK, BLK), 1)
    if cross_made:
        *outs, cross_out = outs
        made = []
        for e in range(4):
            at = 4 * e
            cross = dot(pl.multiple_of(table[at] * BLK, BLK), BLK, pl.multiple_of(table[at + 1] * BLK, BLK))
            made.append(jnp.sum(jnp.where(i == j, cross, 0.0), axis=0, keepdims=True))
        lines = jnp.concatenate(made + [jnp.zeros((EXTRA - 4, BLK), F32)], axis=0)
        cross_out[...] = lines

    for out, (first, count, row0, rows, ring, added) in zip(outs, plan):

        def plus(o, value, rows=rows, ring=ring, added=added):
            for n, at in added:
                if ring:
                    term = terms[n][pl.ds(pl.multiple_of((at + o) * rows, 16), rows), :]
                else:
                    term = terms[n][at + o]
                value = value + term.astype(F32)
            return value

        def put(o, value, out=out, rows=rows, ring=ring):
            if ring:
                out[pl.ds(pl.multiple_of(o * rows, 16), rows), :] = value
            else:
                out[o] = value

        batch = 8 if count % 8 == 0 else 4

        @pl.loop(0, count // batch)
        def _(g, batch=batch, first=first, row0=row0, rows=rows, put=put, plus=plus, out=out):
            starts, values = [], []
            for u in range(batch):
                at = 4 * (first + g * batch + u)
                rows_at = pl.multiple_of(table[at] * BLK + row0, 16)
                starts.append(rows_at)
                value = dot(rows_at, rows, pl.multiple_of(table[at + 1] * BLK, BLK))
                values.append(plus(g * batch + u, value).astype(out.dtype))
            for u in range(batch):
                put(g * batch + u, values[u])
            for u in range(batch):
                at = 4 * (first + g * batch + u)

                @pl.when(table[at + 3] == 1)
                def _(u=u, at=at):
                    cols_at = pl.multiple_of(table[at + 1] * BLK, BLK)
                    mixed_at = pl.multiple_of(table[at + 2] * BLK, BLK)
                    value = dot(starts[u], rows, cols_at)
                    mixed = dot(starts[u], rows, mixed_at)
                    low = i[:rows] + row0 >= j[:rows]
                    value = plus(g * batch + u, jnp.where(low, value, mixed))
                    put(g * batch + u, value.astype(out.dtype))

        if ring:
            total = lines
            for n, _ in added:
                total = total + terms[n][pl.ds(16 * REST, EXTRA), :].astype(F32)
            out[pl.ds(count * rows, EXTRA), :] = total.astype(out.dtype)


def products(operands, table, plan, kinds, cross=None, cross_made=False, terms=(), weight=1):
    shapes = []
    for (_, count, _, rows, ring, _), kind in zip(plan, kinds):
        shape = (count * rows + EXTRA, BLK) if ring else (count, rows, BLK)
        shapes.append(jax.ShapeDtypeStruct(shape, kind))
    if cross_made:
        shapes.append(jax.ShapeDtypeStruct((EXTRA, BLK), F32))
    vmem = pl.BlockSpec(memory_space=pltpu.VMEM)
    opening = len(operands) == 6
    if opening:
        half, deep = operands[0].shape
        shapes += [jax.ShapeDtypeStruct((2 * half, 2 * deep), BF), jax.ShapeDtypeStruct((2 * deep, 2 * half), BF)]
    extra = () if cross is None else (cross,)
    return pl.pallas_call(
        functools.partial(product_kernel, plan, opening, cross_made, cross is not None),
        out_shape=shapes,
        in_specs=[pl.BlockSpec(memory_space=pltpu.SMEM)] + [vmem] * (len(operands) + len(extra) + len(terms)),
        out_specs=[vmem] * len(shapes),
        scratch_shapes=[pltpu.SemaphoreType.DMA((6,))] if opening else [],
        compiler_params=grant(24),
        cost_estimate=cost(weight),
    )(table, *operands, *extra, *terms)


def call_sum(kernel, shapes, *operands):
    vmem = pl.BlockSpec(memory_space=pltpu.VMEM)
    return pl.pallas_call(
        kernel,
        out_shape=[jax.ShapeDtypeStruct(shape, kind) for shape, kind in shapes],
        in_specs=[vmem] * len(operands),
        out_specs=[vmem] * len(shapes),
        compiler_params=grant(12),
        cost_estimate=cost(1),
    )(*operands)


def add_kernel(own, got, out):
    out[...] = (own[...] + got[...].astype(F32)).astype(out.dtype)


def home_kernel(*refs):
    homes, (got_3p, got_2m, got_2p, got_3m), outs = refs[:4], refs[4:8], refs[8:]
    for d, (home, out) in enumerate(zip(homes, outs)):
        one, two = (got_3p, got_2m) if d < 2 else (got_2p, got_3m)
        half = pl.ds(4 * (d % 2), 4)
        out[...] = (home[...] + one[half].astype(F32) + two[half].astype(F32)).astype(out.dtype)


def home_rest_kernel(*refs):
    homes, got, outs = refs[:4], refs[4], refs[5:]
    quarter = homes[0].shape[0] - EXTRA
    for d, (home, out) in enumerate(zip(homes, outs)):
        out[pl.ds(0, quarter), :] = (
            home[pl.ds(0, quarter), :] + got[pl.ds(d * quarter, quarter), :].astype(F32)
        ).astype(out.dtype)
        out[pl.ds(quarter, EXTRA), :] = (
            home[pl.ds(quarter, EXTRA), :] + got[pl.ds(4 * quarter, EXTRA), :].astype(F32)
        ).astype(out.dtype)


def main_sum_kernel(own, second, first, third, *outs):
    for d, out in enumerate(outs):
        total = own[d]
        for ref in (second, first, third):
            total = total + ref[d].astype(F32)
        out[...] = total


def rest_sum_kernel(own, second, first, third, *outs):
    quarter = own.shape[0] - EXTRA
    cross = own[pl.ds(quarter, EXTRA), :][0:1]
    for d, ref in ((2, second), (1, first), (3, third)):
        cross = cross + ref[pl.ds(quarter, EXTRA), :].astype(F32)[d : d + 1]
    cross = jnp.broadcast_to(cross, (8, BLK))
    for d, out in enumerate(outs):
        part = pl.ds(d * REST, REST)
        total = own[part, :]
        for ref in (second, first, third):
            total = total + ref[part, :].astype(F32)
        out[pl.ds(0, REST), :] = total
        out[pl.ds(REST, 8), :] = cross


def last_sum_kernel(own, second, first, third, out, sent):
    total = own[...] + second[...] + first[...] + third[...]
    out[...] = total
    sent[...] = total[: sent.shape[0]].astype(sent.dtype)


def finish_kernel(state, scale, main_ref, rest_ref, got_main_ref, got_rest_ref, out_ref):
    s, fold = state[0], state[1]
    here = jnp.concatenate([main_ref[...], rest_ref[0:REST, :]], axis=0) * scale
    got = jnp.concatenate([got_main_ref[...], got_rest_ref[...]], axis=0).T.astype(F32) * scale
    first_at, second_at = pl.multiple_of(s * BLK, BLK), pl.multiple_of((1 - s) * BLK, BLK)

    @pl.when(fold == 0)
    def _():
        out_ref[:, pl.ds(first_at, BLK)] = here
        out_ref[:, pl.ds(second_at, BLK)] = got

    @pl.when(fold == 1)
    def _():
        i = lax.broadcasted_iota(jnp.int32, (BLK, BLK), 0)
        j = lax.broadcasted_iota(jnp.int32, (BLK, BLK), 1)
        cross = rest_ref[REST : REST + 1, :] * scale
        out_ref[:, pl.ds(first_at, BLK)] = jnp.where(i >= j, here, here.T)
        out_ref[:, pl.ds(second_at, BLK)] = jnp.where(i == j, cross, jnp.where(i > j, got, here))


def local(design, weight, counts, column_map):
    rows_here = design.shape[0]
    core = lax.axis_index("core")
    place = {name: lax.axis_index(name) for name in ("z", "y", "x")}
    total_rows = rows_here * 128

    own_low, own_high = scaled_rows(column_map, counts, weight, design)

    def move(array, pairs):
        return lax.ppermute(array, AXES, pairs)

    M, R = MAIN_ORDER, REST_ORDER

    def main_to(stage, step):
        return shift_pairs(*M, stage, step)

    def rest_to(stage, step):
        return shift_pairs(*R, stage, step)

    swap = [(0, 1), (1, 0)]
    other_low = lax.ppermute(own_low, "core", swap)
    other_high = lax.ppermute(own_high, "core", swap)
    half = own_low.shape
    own_turned, low_turned = pl.pallas_call(
        turn_kernel,
        out_shape=[
            jax.ShapeDtypeStruct((half[1], 2 * half[0]), BF),
            jax.ShapeDtypeStruct((half[1], half[0]), BF),
        ],
        in_specs=[pl.BlockSpec(memory_space=pltpu.VMEM)] * 3,
        out_specs=[pl.BlockSpec(memory_space=pltpu.VMEM)] * 2,
        compiler_params=grant(12),
        cost_estimate=cost(1),
    )(own_low, own_high, other_low)

    plus = [(a, b) for a in (0, 1) for b in range(4)]
    minus = [(a, b) for a in (2, 3) for b in range(4)]
    every = plus + minus
    tables = [cross_table()]

    def blocks(order, d, rest, *added):
        first = sum(t.shape[1] for t in tables) // 4
        tables.append(block_table(order, [(d,) + p for p in rest]))
        row0, rows = (0, MAIN) if order is M else (MAIN, REST)
        return first, len(rest), row0, rows, order is R, added

    plan_1 = [blocks(M, 2, plus), blocks(M, 2, minus)]
    plan_1r = [blocks(R, 3, every)]
    plan_2 = [blocks(M, 1, minus), blocks(M, 3, plus)]
    plan_2r = [blocks(R, 2, every, (0, 0))]
    plan_3 = [blocks(M, 1, plus, (0, 0)), blocks(M, 3, minus, (1, 0))]
    plan_3r = [blocks(R, 1, every)]
    plan_4 = [
        blocks(M, 0, every[4 * d : 4 * d + 4])
        for d in range(4)
    ]
    plan_4r = [blocks(R, 0, every[4 * d : 4 * d + 4]) for d in range(4)]
    device = ((place["z"] * 4 + place["y"]) * 4 + place["x"]) * 2 + core
    table = lax.dynamic_index_in_dim(
        jnp.asarray(np.concatenate(tables, axis=1)), device, 0, keepdims=False
    )

    pieces = (own_low, own_high, other_low, other_high, own_turned, low_turned)
    ring, cross, *both = products(pieces, table, plan_1r, (BF,), cross_made=True)
    got_r = move(ring, rest_to(0, 1))
    first_p, first_m = products(both, table, plan_1, (BF, BF))
    got_1p = move(first_p, main_to(0, 1))
    got_1m = move(first_m, main_to(0, -1))
    both, first_p = lax.optimization_barrier((both, first_p))
    side_p, side_m = products(both, table, plan_2, (BF, BF))
    got_2p = move(side_p, main_to(0, 1))
    got_2m = move(side_m, main_to(0, -1))
    both, side_p = lax.optimization_barrier((both, side_p))
    (ring,) = products(both, table, plan_2r, (BF,), cross, terms=(got_r,))
    got_r = move(ring, rest_to(0, 1))
    both, ring = lax.optimization_barrier((both, ring))
    relay_p, relay_m = products(both, table, plan_3, (BF, BF), terms=(got_1p, got_1m))
    got_3p = move(relay_p, main_to(0, 1))
    got_3m = move(relay_m, main_to(0, -1))
    both, relay_p, got_2p, got_2m = lax.optimization_barrier((both, relay_p, got_2p, got_2m))
    (line,) = products(both, table, plan_3r, (F32,), cross, weight=WEIGHT)
    (ring,) = call_sum(add_kernel, [(line.shape, BF)], line, got_r)
    got_r = move(ring, rest_to(0, 1))
    both, ring = lax.optimization_barrier((both, ring))
    home = products(both, table, plan_4, (F32,) * 4, weight=WEIGHT)
    both, home = lax.optimization_barrier((both, home))
    line = products(both, table, plan_4r, (F32,) * 4, cross, weight=WEIGHT)
    part = call_sum(
        home_kernel, [(h.shape, F32 if d == 0 else BF) for d, h in enumerate(home)], *home, got_3p, got_2m, got_2p, got_3m
    )
    rest = call_sum(home_rest_kernel, [(h.shape, F32 if d == 0 else BF) for d, h in enumerate(line)], *line, got_r)

    got = [move(part[d], main_to(1, d)) for d in (2, 1, 3)]
    got_r = [move(rest[d], rest_to(1, d)) for d in (2, 1, 3)]
    part = call_sum(main_sum_kernel, [((MAIN, BLK), F32)] * 4, part[0], *got)
    rest = call_sum(rest_sum_kernel, [((REST + 8, BLK), F32)] * 4, rest[0], *got_r)

    got = [move(part[d], main_to(2, d)) for d in (2, 1, 3)]
    got_r = [move(rest[d], rest_to(2, d)) for d in (2, 1, 3)]
    main_3, main_sent = call_sum(last_sum_kernel, [((MAIN, BLK), F32), ((MAIN, BLK), BF)], part[0], *got)
    rest_3, rest_sent = call_sum(last_sum_kernel, [((REST + 8, BLK), F32), ((REST, BLK), BF)], rest[0], *got_r)
    got_main = move(main_sent, mirror_pairs())
    got_rest = move(rest_sent, mirror_pairs())

    r, c = 4 * place["z"] + place["y"], 2 * place["x"] + core
    i, h = r // 2, r % 2
    s = jnp.where(i <= c, h, 1 - h)
    state = jnp.stack([s, (i == c).astype(jnp.int32)]).astype(jnp.int32)
    vmem = pl.BlockSpec(memory_space=pltpu.VMEM)
    return pl.pallas_call(
        lambda *refs: finish_kernel(refs[0], 1.0 / total_rows, *refs[1:]),
        out_shape=jax.ShapeDtypeStruct((BLK, 2 * BLK), F32),
        in_specs=[pl.BlockSpec(memory_space=pltpu.SMEM)] + [vmem] * 4,
        out_specs=vmem,
        compiler_params=pltpu.CompilerParams(vmem_limit_bytes=16 * 1024 * 1024),
    )(state, main_3, rest_3, got_main, got_rest)


def solution(mesh):
    fine = Mesh(mesh.devices.reshape(4, 4, 4, 2), AXES)
    return jax.shard_map(
        local,
        mesh=fine,
        in_specs=(P(AXES, None), P(AXES), P(AXES), P()),
        out_specs=P(("z", "y"), ("x", "core")),
        check_vma=False,
    )
```

```python
import functools

import jax
import jax.numpy as jnp
import numpy as np
from jax import lax
from jax.experimental import pallas as pl
from jax.experimental.pallas import tpu as pltpu
from jax.sharding import Mesh, PartitionSpec as P

ARC_ROWS = 32
AXES = ("z", "y", "x", "core")
BLK = 256
MAIN = 176
REST = BLK - MAIN
GRANT_FIRST = 24
WEIGHT = 20
EXTRA = 16
BF = jnp.bfloat16
F32 = jnp.float32


def linear(z, y, x, q):
    return ((z % 4 * 4 + y % 4) * 4 + x % 4) * 2 + q


def shift_pairs(order0, order1, sign1, stage, step):
    pairs = []
    for z in range(4):
        for y in range(4):
            for x in range(4):
                for q in range(2):
                    axis = (order0, order1)[q][stage]
                    by = step * (1, sign1)[q]
                    to = {"z": z, "y": y, "x": x}
                    to[axis] += by
                    pairs.append((linear(z, y, x, q), linear(to["z"], to["y"], to["x"], q)))
    return pairs


def mirror_pairs():
    pairs = []
    for z in range(4):
        for y in range(4):
            for x in range(4):
                for q in range(2):
                    r, c = 4 * z + y, 2 * x + q
                    i, h = r // 2, r % 2
                    if i < c:
                        to_r, to_c = 2 * c + h, i
                    elif i > c:
                        to_r, to_c = 2 * c + 1 - h, i
                    else:
                        to_r, to_c = 2 * i + 1 - h, i
                    to = linear(to_r // 4, to_r % 4, to_c // 2, to_c % 2)
                    pairs.append((linear(z, y, x, q), to))
    return pairs


MAIN_ORDER = (("x", "z", "y"), ("z", "y", "x"), 1)
REST_ORDER = (("y", "x", "z"), ("y", "x", "z"), -1)


def block_table(order, offsets):
    order0, order1, sign1 = order
    rows = []
    for device in range(128):
        place = {"z": device // 32, "y": device // 8 % 4, "x": device // 2 % 4}
        core = device % 2
        for d in offsets:
            at = dict(place)
            for name, by in zip((order0, order1)[core], d):
                at[name] = (place[name] + by * (1, sign1)[core]) % 4
            r, c = 4 * at["z"] + at["y"], 2 * at["x"] + core
            i, h = r // 2, r % 2
            s = h if i <= c else 1 - h
            rows += [r, 2 * c + s, 2 * c + 1 - s, int(i == c)]
    return np.asarray(rows, np.int32).reshape(128, -1)


def cross_table():
    rows = []
    for device in range(128):
        x, core = device // 2 % 4, device % 2
        for d in range(4):
            first = 2 * (2 * ((x + d * (1, REST_ORDER[2])[core]) % 4) + core)
            rows += [first, first + 1, 0, 0]
    return np.asarray(rows, np.int32).reshape(128, -1)


def pick_rows(map_ref, first, columns, picked, out_ref):
    width, half, unroll = out_ref.shape[1], out_ref.shape[1] // 2, 32

    @pl.loop(0, out_ref.shape[0] // unroll)
    def _(g):
        rows = [columns[pl.ds(2 * map_ref[first + g * unroll + u], 2), :] for u in range(unroll)]
        for u in range(unroll):
            picked[pl.ds(2 * (g * unroll + u), 2), :] = rows[u]

    @pl.loop(0, out_ref.shape[0] // width)
    def _(t):
        at = pl.multiple_of(t * width, width)
        for h in range(2):
            out_ref[pl.ds(at, width), pl.ds(h * half, half)] = picked[
                pl.ds(2 * at + h, width, 2), :
            ].astype(BF)


def first_pick_kernel(map_ref, counts_ref, weight_ref, design_ref, columns, out_ref, held, picked, sems):
    width, half = held.shape[0], held.shape[0] // 2
    tiles, loads = held.shape[1] // width, sems.shape[0]
    copies = []
    for n in range(loads):
        part = pl.ds(n * (held.shape[1] // loads), held.shape[1] // loads)
        copies.append(pltpu.make_async_copy(design_ref.at[:, part], held.at[:, part], sems.at[n]))
        copies[-1].start()

    slot = lax.broadcasted_iota(jnp.int32, (1, width), 1)
    count = jnp.zeros((1, width), jnp.int32)
    for arc in range(width // ARC_ROWS):
        count = jnp.where(slot // ARC_ROWS == arc, counts_ref[arc], count)
    weight = weight_ref[...]
    scale = jnp.sqrt(jnp.where(slot % ARC_ROWS < count, weight, jnp.zeros_like(weight)))

    for n in range(loads):
        copies[n].wait()

        @pl.loop(n * (tiles // loads), (n + 1) * (tiles // loads))
        def _(t):
            at = pl.multiple_of(t * width, width)
            wide = (held[:, pl.ds(at, width)].T.astype(F32) * scale).astype(BF).astype(F32)
            for h in range(2):
                columns[pl.ds(2 * at + h, width, 2), :] = wide[:, h * half : (h + 1) * half]

    pick_rows(map_ref, 0, columns, picked, out_ref)


def second_pick_kernel(map_ref, columns, out_ref, picked):
    pick_rows(map_ref, out_ref.shape[0], columns, picked, out_ref)


def cost(size):
    return pl.CostEstimate(flops=0, bytes_accessed=size << 20, transcendentals=0)


def grant(size):
    return pltpu.CompilerParams(vmem_limit_bytes=size * 1024 * 1024)


def scaled_rows(column_map, counts, weight, design):
    rows, unknowns = design.shape
    vmem, smem = pl.BlockSpec(memory_space=pltpu.VMEM), pl.BlockSpec(memory_space=pltpu.SMEM)
    part = jax.ShapeDtypeStruct((unknowns // 2, rows), BF)
    picked = pltpu.VMEM((unknowns, rows // 2), F32)
    columns, low = pl.pallas_call(
        first_pick_kernel,
        out_shape=[jax.ShapeDtypeStruct((2 * unknowns, rows // 2), F32), part],
        in_specs=[smem, smem, vmem, pl.BlockSpec(memory_space=pl.ANY)],
        out_specs=[vmem, vmem],
        scratch_shapes=[pltpu.VMEM((rows, unknowns), BF), picked, pltpu.SemaphoreType.DMA((4,))],
        compiler_params=grant(GRANT_FIRST),
        cost_estimate=cost(8),
    )(column_map, counts, weight[None, :], design)
    high = pl.pallas_call(
        second_pick_kernel,
        out_shape=part,
        in_specs=[smem, vmem],
        out_specs=vmem,
        scratch_shapes=[picked],
        compiler_params=grant(16),
        cost_estimate=cost(8),
    )(column_map, columns)
    return low, high


def turn(from_ref, to_ref, row, column):
    deep = from_ref.shape[1]

    @pl.loop(0, from_ref.shape[0] // BLK)
    def _(t):
        at = pl.multiple_of(t * BLK, BLK)
        to_ref[pl.ds(row, deep), pl.ds(column + at, BLK)] = from_ref[pl.ds(at, BLK), :].T


def turn_kernel(own_low, own_high, other_low, own_out, low_out):
    turn(own_low, own_out, 0, 0)
    turn(own_high, own_out, 0, own_low.shape[0])
    turn(other_low, low_out, 0, 0)


def product_kernel(plan, opening, cross_made, cross_used, table, *refs):
    if opening:
        own_low, own_high, other_low, other_high, own_turned, low_turned, *outs, sems = refs
        *outs, held, turned = outs
        terms, lines = [], None
        half, deep = own_low.shape
        pieces = [
            (own_low, held.at[pl.ds(0, half), pl.ds(0, deep)]),
            (own_high, held.at[pl.ds(half, half), pl.ds(0, deep)]),
            (other_low, held.at[pl.ds(0, half), pl.ds(deep, deep)]),
            (other_high, held.at[pl.ds(half, half), pl.ds(deep, deep)]),
            (own_turned, turned.at[pl.ds(0, deep), :]),
            (low_turned, turned.at[pl.ds(deep, deep), pl.ds(0, half)]),
        ]
        copies = [pltpu.make_async_copy(a, b, sems.at[n]) for n, (a, b) in enumerate(pieces)]
        for copy in copies:
            copy.start()
        turn(other_high, turned, deep, half)
        for copy in copies:
            copy.wait()
    else:
        held, turned, *outs = refs
        lines = None
        if cross_used:
            lines, *outs = outs
            lines = lines[...]
        count = len(outs) - len(plan) - int(cross_made)
        terms, outs = outs[:count], outs[count:]

    def dot(rows_at, rows, cols_at):
        return jnp.dot(
            held[pl.ds(rows_at, rows), :], turned[:, pl.ds(cols_at, BLK)], preferred_element_type=F32
        )

    i = lax.broadcasted_iota(jnp.int32, (BLK, BLK), 0)
    j = lax.broadcasted_iota(jnp.int32, (BLK, BLK), 1)
    if cross_made:
        *outs, cross_out = outs
        made = []
        for e in range(4):
            at = 4 * e
            cross = dot(pl.multiple_of(table[at] * BLK, BLK), BLK, pl.multiple_of(table[at + 1] * BLK, BLK))
            made.append(jnp.sum(jnp.where(i == j, cross, 0.0), axis=0, keepdims=True))
        lines = jnp.concatenate(made + [jnp.zeros((EXTRA - 4, BLK), F32)], axis=0)
        cross_out[...] = lines

    for out, (first, count, row0, rows, ring, added) in zip(outs, plan):

        def plus(o, value, rows=rows, ring=ring, added=added):
            for n, at in added:
                if ring:
                    term = terms[n][pl.ds(pl.multiple_of((at + o) * rows, 16), rows), :]
                else:
                    term = terms[n][at + o]
                value = value + term.astype(F32)
            return value

        def put(o, value, out=out, rows=rows, ring=ring):
            if ring:
                out[pl.ds(pl.multiple_of(o * rows, 16), rows), :] = value
            else:
                out[o] = value

        batch = 8 if count % 8 == 0 else 4

        @pl.loop(0, count // batch)
        def _(g, batch=batch, first=first, row0=row0, rows=rows, put=put, plus=plus, out=out):
            starts, values = [], []
            for u in range(batch):
                at = 4 * (first + g * batch + u)
                rows_at = pl.multiple_of(table[at] * BLK + row0, 16)
                starts.append(rows_at)
                value = dot(rows_at, rows, pl.multiple_of(table[at + 1] * BLK, BLK))
                values.append(plus(g * batch + u, value).astype(out.dtype))
            for u in range(batch):
                put(g * batch + u, values[u])
            for u in range(batch):
                at = 4 * (first + g * batch + u)

                @pl.when(table[at + 3] == 1)
                def _(u=u, at=at):
                    cols_at = pl.multiple_of(table[at + 1] * BLK, BLK)
                    mixed_at = pl.multiple_of(table[at + 2] * BLK, BLK)
                    value = dot(starts[u], rows, cols_at)
                    mixed = dot(starts[u], rows, mixed_at)
                    low = i[:rows] + row0 >= j[:rows]
                    value = plus(g * batch + u, jnp.where(low, value, mixed))
                    put(g * batch + u, value.astype(out.dtype))

        if ring:
            total = lines
            for n, _ in added:
                total = total + terms[n][pl.ds(16 * REST, EXTRA), :].astype(F32)
            out[pl.ds(count * rows, EXTRA), :] = total.astype(out.dtype)


def products(operands, table, plan, kinds, cross=None, cross_made=False, terms=(), weight=1):
    shapes = []
    for (_, count, _, rows, ring, _), kind in zip(plan, kinds):
        shape = (count * rows + EXTRA, BLK) if ring else (count, rows, BLK)
        shapes.append(jax.ShapeDtypeStruct(shape, kind))
    if cross_made:
        shapes.append(jax.ShapeDtypeStruct((EXTRA, BLK), F32))
    vmem = pl.BlockSpec(memory_space=pltpu.VMEM)
    opening = len(operands) == 6
    if opening:
        half, deep = operands[0].shape
        shapes += [jax.ShapeDtypeStruct((2 * half, 2 * deep), BF), jax.ShapeDtypeStruct((2 * deep, 2 * half), BF)]
    extra = () if cross is None else (cross,)
    return pl.pallas_call(
        functools.partial(product_kernel, plan, opening, cross_made, cross is not None),
        out_shape=shapes,
        in_specs=[pl.BlockSpec(memory_space=pltpu.SMEM)] + [vmem] * (len(operands) + len(extra) + len(terms)),
        out_specs=[vmem] * len(shapes),
        scratch_shapes=[pltpu.SemaphoreType.DMA((6,))] if opening else [],
        compiler_params=grant(24),
        cost_estimate=cost(weight),
    )(table, *operands, *extra, *terms)


def call_sum(kernel, shapes, *operands):
    vmem = pl.BlockSpec(memory_space=pltpu.VMEM)
    return pl.pallas_call(
        kernel,
        out_shape=[jax.ShapeDtypeStruct(shape, kind) for shape, kind in shapes],
        in_specs=[vmem] * len(operands),
        out_specs=[vmem] * len(shapes),
        compiler_params=grant(12),
        cost_estimate=cost(1),
    )(*operands)


def add_kernel(own, got, out):
    out[...] = (own[...] + got[...].astype(F32)).astype(out.dtype)


def home_kernel(*refs):
    homes, (got_3p, got_2m, got_2p, got_3m), outs = refs[:4], refs[4:8], refs[8:]
    for d, (home, out) in enumerate(zip(homes, outs)):
        one, two = (got_3p, got_2m) if d < 2 else (got_2p, got_3m)
        half = pl.ds(4 * (d % 2), 4)
        out[...] = (home[...] + one[half].astype(F32) + two[half].astype(F32)).astype(out.dtype)


def home_rest_kernel(*refs):
    homes, got, outs = refs[:4], refs[4], refs[5:]
    quarter = homes[0].shape[0] - EXTRA
    for d, (home, out) in enumerate(zip(homes, outs)):
        out[pl.ds(0, quarter), :] = (
            home[pl.ds(0, quarter), :] + got[pl.ds(d * quarter, quarter), :].astype(F32)
        ).astype(out.dtype)
        out[pl.ds(quarter, EXTRA), :] = (
            home[pl.ds(quarter, EXTRA), :] + got[pl.ds(4 * quarter, EXTRA), :].astype(F32)
        ).astype(out.dtype)


def main_sum_kernel(own, second, first, third, *outs):
    for d, out in enumerate(outs):
        total = own[d]
        for ref in (second, first, third):
            total = total + ref[d].astype(F32)
        out[...] = total


def rest_sum_kernel(own, second, first, third, *outs):
    quarter = own.shape[0] - EXTRA
    cross = own[pl.ds(quarter, EXTRA), :][0:1]
    for d, ref in ((2, second), (1, first), (3, third)):
        cross = cross + ref[pl.ds(quarter, EXTRA), :].astype(F32)[d : d + 1]
    cross = jnp.broadcast_to(cross, (8, BLK))
    for d, out in enumerate(outs):
        part = pl.ds(d * REST, REST)
        total = own[part, :]
        for ref in (second, first, third):
            total = total + ref[part, :].astype(F32)
        out[pl.ds(0, REST), :] = total
        out[pl.ds(REST, 8), :] = cross


def last_sum_kernel(own, second, first, third, out, sent):
    total = own[...] + second[...] + first[...] + third[...]
    out[...] = total
    sent[...] = total[: sent.shape[0]].astype(sent.dtype)


def finish_kernel(state, scale, main_ref, rest_ref, got_main_ref, got_rest_ref, out_ref):
    s, fold = state[0], state[1]
    here = jnp.concatenate([main_ref[...], rest_ref[0:REST, :]], axis=0) * scale
    got = jnp.concatenate([got_main_ref[...], got_rest_ref[...]], axis=0).T.astype(F32) * scale
    first_at, second_at = pl.multiple_of(s * BLK, BLK), pl.multiple_of((1 - s) * BLK, BLK)

    @pl.when(fold == 0)
    def _():
        out_ref[:, pl.ds(first_at, BLK)] = here
        out_ref[:, pl.ds(second_at, BLK)] = got

    @pl.when(fold == 1)
    def _():
        i = lax.broadcasted_iota(jnp.int32, (BLK, BLK), 0)
        j = lax.broadcasted_iota(jnp.int32, (BLK, BLK), 1)
        cross = rest_ref[REST : REST + 1, :] * scale
        out_ref[:, pl.ds(first_at, BLK)] = jnp.where(i >= j, here, here.T)
        out_ref[:, pl.ds(second_at, BLK)] = jnp.where(i == j, cross, jnp.where(i > j, got, here))


def local(design, weight, counts, column_map):
    rows_here = design.shape[0]
    core = lax.axis_index("core")
    place = {name: lax.axis_index(name) for name in ("z", "y", "x")}
    total_rows = rows_here * 128

    own_low, own_high = scaled_rows(column_map, counts, weight, design)

    def move(array, pairs):
        return lax.ppermute(array, AXES, pairs)

    M, R = MAIN_ORDER, REST_ORDER

    def main_to(stage, step):
        return shift_pairs(*M, stage, step)

    def rest_to(stage, step):
        return shift_pairs(*R, stage, step)

    swap = [(0, 1), (1, 0)]
    other_low = lax.ppermute(own_low, "core", swap)
    other_high = lax.ppermute(own_high, "core", swap)
    half = own_low.shape
    own_turned, low_turned = pl.pallas_call(
        turn_kernel,
        out_shape=[
            jax.ShapeDtypeStruct((half[1], 2 * half[0]), BF),
            jax.ShapeDtypeStruct((half[1], half[0]), BF),
        ],
        in_specs=[pl.BlockSpec(memory_space=pltpu.VMEM)] * 3,
        out_specs=[pl.BlockSpec(memory_space=pltpu.VMEM)] * 2,
        compiler_params=grant(12),
        cost_estimate=cost(1),
    )(own_low, own_high, other_low)

    plus = [(a, b) for a in (0, 1) for b in range(4)]
    minus = [(a, b) for a in (2, 3) for b in range(4)]
    every = plus + minus
    tables = [cross_table()]

    def blocks(order, d, rest, *added):
        first = sum(t.shape[1] for t in tables) // 4
        tables.append(block_table(order, [(d,) + p for p in rest]))
        row0, rows = (0, MAIN) if order is M else (MAIN, REST)
        return first, len(rest), row0, rows, order is R, added

    plan_1 = [blocks(M, 2, plus), blocks(M, 2, minus)]
    plan_1r = [blocks(R, 3, every)]
    plan_2 = [blocks(M, 1, minus), blocks(M, 3, plus)]
    plan_2r = [blocks(R, 2, every, (0, 0))]
    plan_3 = [blocks(M, 1, plus, (0, 0)), blocks(M, 3, minus, (1, 0))]
    plan_3r = [blocks(R, 1, every)]
    plan_4 = [
        blocks(M, 0, every[4 * d : 4 * d + 4])
        for d in range(4)
    ]
    plan_4r = [blocks(R, 0, every[4 * d : 4 * d + 4]) for d in range(4)]
    device = ((place["z"] * 4 + place["y"]) * 4 + place["x"]) * 2 + core
    table = lax.dynamic_index_in_dim(
        jnp.asarray(np.concatenate(tables, axis=1)), device, 0, keepdims=False
    )

    pieces = (own_low, own_high, other_low, other_high, own_turned, low_turned)
    ring, cross, *both = products(pieces, table, plan_1r, (BF,), cross_made=True)
    got_r = move(ring, rest_to(0, 1))
    first_p, first_m = products(both, table, plan_1, (BF, BF))
    got_1p = move(first_p, main_to(0, 1))
    got_1m = move(first_m, main_to(0, -1))
    both, first_p = lax.optimization_barrier((both, first_p))
    side_p, side_m = products(both, table, plan_2, (BF, BF))
    got_2p = move(side_p, main_to(0, 1))
    got_2m = move(side_m, main_to(0, -1))
    both, side_p = lax.optimization_barrier((both, side_p))
    (ring,) = products(both, table, plan_2r, (BF,), cross, terms=(got_r,))
    got_r = move(ring, rest_to(0, 1))
    both, ring = lax.optimization_barrier((both, ring))
    relay_p, relay_m = products(both, table, plan_3, (BF, BF), terms=(got_1p, got_1m))
    got_3p = move(relay_p, main_to(0, 1))
    got_3m = move(relay_m, main_to(0, -1))
    both, relay_p, got_2p, got_2m = lax.optimization_barrier((both, relay_p, got_2p, got_2m))
    (line,) = products(both, table, plan_3r, (F32,), cross, weight=WEIGHT)
    (ring,) = call_sum(add_kernel, [(line.shape, BF)], line, got_r)
    got_r = move(ring, rest_to(0, 1))
    both, ring = lax.optimization_barrier((both, ring))
    home = products(both, table, plan_4, (F32,) * 4, weight=WEIGHT)
    both, home = lax.optimization_barrier((both, home))
    line = products(both, table, plan_4r, (F32,) * 4, cross, weight=WEIGHT)
    part = call_sum(
        home_kernel, [(h.shape, F32 if d == 0 else BF) for d, h in enumerate(home)], *home, got_3p, got_2m, got_2p, got_3m
    )
    rest = call_sum(home_rest_kernel, [(h.shape, F32 if d == 0 else BF) for d, h in enumerate(line)], *line, got_r)

    got = [move(part[d], main_to(1, d)) for d in (2, 1, 3)]
    got_r = [move(rest[d], rest_to(1, d)) for d in (2, 1, 3)]
    part = call_sum(main_sum_kernel, [((MAIN, BLK), F32)] * 4, part[0], *got)
    rest = call_sum(rest_sum_kernel, [((REST + 8, BLK), F32)] * 4, rest[0], *got_r)

    got = [move(part[d], main_to(2, d)) for d in (2, 1, 3)]
    got_r = [move(rest[d], rest_to(2, d)) for d in (2, 1, 3)]
    main_3, main_sent = call_sum(last_sum_kernel, [((MAIN, BLK), F32), ((MAIN, BLK), F32)], part[0], *got)
    rest_3, rest_sent = call_sum(last_sum_kernel, [((REST + 8, BLK), F32), ((REST, BLK), F32)], rest[0], *got_r)
    got_main = move(main_sent, mirror_pairs())
    got_rest = move(rest_sent, mirror_pairs())

    r, c = 4 * place["z"] + place["y"], 2 * place["x"] + core
    i, h = r // 2, r % 2
    s = jnp.where(i <= c, h, 1 - h)
    state = jnp.stack([s, (i == c).astype(jnp.int32)]).astype(jnp.int32)
    vmem = pl.BlockSpec(memory_space=pltpu.VMEM)
    return pl.pallas_call(
        lambda *refs: finish_kernel(refs[0], 1.0 / total_rows, *refs[1:]),
        out_shape=jax.ShapeDtypeStruct((BLK, 2 * BLK), F32),
        in_specs=[pl.BlockSpec(memory_space=pltpu.SMEM)] + [vmem] * 4,
        out_specs=vmem,
        compiler_params=pltpu.CompilerParams(vmem_limit_bytes=16 * 1024 * 1024),
    )(state, main_3, rest_3, got_main, got_rest)


def solution(mesh):
    fine = Mesh(mesh.devices.reshape(4, 4, 4, 2), AXES)
    return jax.shard_map(
        local,
        mesh=fine,
        in_specs=(P(AXES, None), P(AXES), P(AXES), P()),
        out_specs=P(("z", "y"), ("x", "core")),
        check_vma=False,
    )
```

```python
import functools

import jax
import jax.numpy as jnp
import numpy as np
from jax import lax
from jax.experimental import pallas as pl
from jax.experimental.pallas import tpu as pltpu
from jax.sharding import Mesh, PartitionSpec as P

ARC_ROWS = 32
AXES = ("z", "y", "x", "core")
BLK = 256
MAIN = 176
REST = BLK - MAIN
GRANT_FIRST = 24
WEIGHT = 20
EXTRA = 16
BF = jnp.bfloat16
F32 = jnp.float32


def linear(z, y, x, q):
    return ((z % 4 * 4 + y % 4) * 4 + x % 4) * 2 + q


def shift_pairs(order0, order1, sign1, stage, step):
    pairs = []
    for z in range(4):
        for y in range(4):
            for x in range(4):
                for q in range(2):
                    axis = (order0, order1)[q][stage]
                    by = step * (1, sign1)[q]
                    to = {"z": z, "y": y, "x": x}
                    to[axis] += by
                    pairs.append((linear(z, y, x, q), linear(to["z"], to["y"], to["x"], q)))
    return pairs


def mirror_pairs():
    pairs = []
    for z in range(4):
        for y in range(4):
            for x in range(4):
                for q in range(2):
                    r, c = 4 * z + y, 2 * x + q
                    i, h = r // 2, r % 2
                    if i < c:
                        to_r, to_c = 2 * c + h, i
                    elif i > c:
                        to_r, to_c = 2 * c + 1 - h, i
                    else:
                        to_r, to_c = 2 * i + 1 - h, i
                    to = linear(to_r // 4, to_r % 4, to_c // 2, to_c % 2)
                    pairs.append((linear(z, y, x, q), to))
    return pairs


MAIN_ORDER = (("x", "z", "y"), ("z", "x", "y"), 1)
REST_ORDER = (("y", "x", "z"), ("y", "z", "x"), -1)


def block_table(order, offsets):
    order0, order1, sign1 = order
    rows = []
    for device in range(128):
        place = {"z": device // 32, "y": device // 8 % 4, "x": device // 2 % 4}
        core = device % 2
        for d in offsets:
            at = dict(place)
            for name, by in zip((order0, order1)[core], d):
                at[name] = (place[name] + by * (1, sign1)[core]) % 4
            r, c = 4 * at["z"] + at["y"], 2 * at["x"] + core
            i, h = r // 2, r % 2
            s = h if i <= c else 1 - h
            rows += [r, 2 * c + s, 2 * c + 1 - s, int(i == c)]
    return np.asarray(rows, np.int32).reshape(128, -1)


def cross_table():
    rows = []
    for device in range(128):
        place = {"z": device // 32, "x": device // 2 % 4}
        core = device % 2
        for d in range(4):
            lead = place[REST_ORDER[core][1]] + d * (1, REST_ORDER[2])[core]
            first = 2 * (2 * (lead % 4) + core)
            rows += [first, first + 1, 0, 0]
    return np.asarray(rows, np.int32).reshape(128, -1)


def pick_rows(map_ref, first, columns, picked, out_ref):
    width, half, unroll = out_ref.shape[1], out_ref.shape[1] // 2, 32

    @pl.loop(0, out_ref.shape[0] // unroll)
    def _(g):
        rows = [columns[pl.ds(2 * map_ref[first + g * unroll + u], 2), :] for u in range(unroll)]
        for u in range(unroll):
            picked[pl.ds(2 * (g * unroll + u), 2), :] = rows[u]

    @pl.loop(0, out_ref.shape[0] // width)
    def _(t):
        at = pl.multiple_of(t * width, width)
        for h in range(2):
            out_ref[pl.ds(at, width), pl.ds(h * half, half)] = picked[
                pl.ds(2 * at + h, width, 2), :
            ].astype(BF)


def first_pick_kernel(map_ref, counts_ref, weight_ref, design_ref, columns, out_ref, held, picked, sems):
    width, half = held.shape[0], held.shape[0] // 2
    tiles, loads = held.shape[1] // width, sems.shape[0]
    copies = []
    for n in range(loads):
        part = pl.ds(n * (held.shape[1] // loads), held.shape[1] // loads)
        copies.append(pltpu.make_async_copy(design_ref.at[:, part], held.at[:, part], sems.at[n]))
        copies[-1].start()

    slot = lax.broadcasted_iota(jnp.int32, (1, width), 1)
    count = jnp.zeros((1, width), jnp.int32)
    for arc in range(width // ARC_ROWS):
        count = jnp.where(slot // ARC_ROWS == arc, counts_ref[arc], count)
    weight = weight_ref[...]
    scale = jnp.sqrt(jnp.where(slot % ARC_ROWS < count, weight, jnp.zeros_like(weight)))

    for n in range(loads):
        copies[n].wait()

        @pl.loop(n * (tiles // loads), (n + 1) * (tiles // loads))
        def _(t):
            at = pl.multiple_of(t * width, width)
            wide = (held[:, pl.ds(at, width)].T.astype(F32) * scale).astype(BF).astype(F32)
            for h in range(2):
                columns[pl.ds(2 * at + h, width, 2), :] = wide[:, h * half : (h + 1) * half]

    pick_rows(map_ref, 0, columns, picked, out_ref)


def second_pick_kernel(map_ref, columns, out_ref, picked):
    pick_rows(map_ref, out_ref.shape[0], columns, picked, out_ref)


def cost(size):
    return pl.CostEstimate(flops=0, bytes_accessed=size << 20, transcendentals=0)


def grant(size):
    return pltpu.CompilerParams(vmem_limit_bytes=size * 1024 * 1024)


def scaled_rows(column_map, counts, weight, design):
    rows, unknowns = design.shape
    vmem, smem = pl.BlockSpec(memory_space=pltpu.VMEM), pl.BlockSpec(memory_space=pltpu.SMEM)
    part = jax.ShapeDtypeStruct((unknowns // 2, rows), BF)
    picked = pltpu.VMEM((unknowns, rows // 2), F32)
    columns, low = pl.pallas_call(
        first_pick_kernel,
        out_shape=[jax.ShapeDtypeStruct((2 * unknowns, rows // 2), F32), part],
        in_specs=[smem, smem, vmem, pl.BlockSpec(memory_space=pl.ANY)],
        out_specs=[vmem, vmem],
        scratch_shapes=[pltpu.VMEM((rows, unknowns), BF), picked, pltpu.SemaphoreType.DMA((4,))],
        compiler_params=grant(GRANT_FIRST),
        cost_estimate=cost(8),
    )(column_map, counts, weight[None, :], design)
    high = pl.pallas_call(
        second_pick_kernel,
        out_shape=part,
        in_specs=[smem, vmem],
        out_specs=vmem,
        scratch_shapes=[picked],
        compiler_params=grant(16),
        cost_estimate=cost(8),
    )(column_map, columns)
    return low, high


def turn(from_ref, to_ref, row, column):
    deep = from_ref.shape[1]

    @pl.loop(0, from_ref.shape[0] // BLK)
    def _(t):
        at = pl.multiple_of(t * BLK, BLK)
        to_ref[pl.ds(row, deep), pl.ds(column + at, BLK)] = from_ref[pl.ds(at, BLK), :].T


def turn_kernel(own_low, own_high, other_low, own_out, low_out):
    turn(own_low, own_out, 0, 0)
    turn(own_high, own_out, 0, own_low.shape[0])
    turn(other_low, low_out, 0, 0)


def product_kernel(plan, opening, cross_made, cross_used, table, *refs):
    if opening:
        own_low, own_high, other_low, other_high, own_turned, low_turned, *outs, sems = refs
        *outs, held, turned = outs
        terms, lines = [], None
        half, deep = own_low.shape
        pieces = [
            (own_low, held.at[pl.ds(0, half), pl.ds(0, deep)]),
            (own_high, held.at[pl.ds(half, half), pl.ds(0, deep)]),
            (other_low, held.at[pl.ds(0, half), pl.ds(deep, deep)]),
            (other_high, held.at[pl.ds(half, half), pl.ds(deep, deep)]),
            (own_turned, turned.at[pl.ds(0, deep), :]),
            (low_turned, turned.at[pl.ds(deep, deep), pl.ds(0, half)]),
        ]
        copies = [pltpu.make_async_copy(a, b, sems.at[n]) for n, (a, b) in enumerate(pieces)]
        for copy in copies:
            copy.start()
        turn(other_high, turned, deep, half)
        for copy in copies:
            copy.wait()
    else:
        held, turned, *outs = refs
        lines = None
        if cross_used:
            lines, *outs = outs
            lines = lines[...]
        count = len(outs) - len(plan) - int(cross_made)
        terms, outs = outs[:count], outs[count:]

    def dot(rows_at, rows, cols_at):
        return jnp.dot(
            held[pl.ds(rows_at, rows), :], turned[:, pl.ds(cols_at, BLK)], preferred_element_type=F32
        )

    i = lax.broadcasted_iota(jnp.int32, (BLK, BLK), 0)
    j = lax.broadcasted_iota(jnp.int32, (BLK, BLK), 1)
    if cross_made:
        *outs, cross_out = outs
        made = []
        for e in range(4):
            at = 4 * e
            cross = dot(pl.multiple_of(table[at] * BLK, BLK), BLK, pl.multiple_of(table[at + 1] * BLK, BLK))
            made.append(jnp.sum(jnp.where(i == j, cross, 0.0), axis=0, keepdims=True))
        lines = jnp.concatenate(made + [jnp.zeros((EXTRA - 4, BLK), F32)], axis=0)
        cross_out[...] = lines

    for out, (first, count, row0, rows, ring, added) in zip(outs, plan):

        def plus(o, value, rows=rows, ring=ring, added=added):
            for n, at in added:
                if ring:
                    term = terms[n][pl.ds(pl.multiple_of((at + o) * rows, 16), rows), :]
                else:
                    term = terms[n][at + o]
                value = value + term.astype(F32)
            return value

        def put(o, value, out=out, rows=rows, ring=ring):
            if ring:
                out[pl.ds(pl.multiple_of(o * rows, 16), rows), :] = value
            else:
                out[o] = value

        batch = 8 if count % 8 == 0 else 4

        @pl.loop(0, count // batch)
        def _(g, batch=batch, first=first, row0=row0, rows=rows, put=put, plus=plus, out=out):
            starts, values = [], []
            for u in range(batch):
                at = 4 * (first + g * batch + u)
                rows_at = pl.multiple_of(table[at] * BLK + row0, 16)
                starts.append(rows_at)
                value = dot(rows_at, rows, pl.multiple_of(table[at + 1] * BLK, BLK))
                values.append(plus(g * batch + u, value).astype(out.dtype))
            for u in range(batch):
                put(g * batch + u, values[u])
            for u in range(batch):
                at = 4 * (first + g * batch + u)

                @pl.when(table[at + 3] == 1)
                def _(u=u, at=at):
                    cols_at = pl.multiple_of(table[at + 1] * BLK, BLK)
                    mixed_at = pl.multiple_of(table[at + 2] * BLK, BLK)
                    value = dot(starts[u], rows, cols_at)
                    mixed = dot(starts[u], rows, mixed_at)
                    low = i[:rows] + row0 >= j[:rows]
                    value = plus(g * batch + u, jnp.where(low, value, mixed))
                    put(g * batch + u, value.astype(out.dtype))

        if ring:
            total = lines
            for n, _ in added:
                total = total + terms[n][pl.ds(16 * REST, EXTRA), :].astype(F32)
            out[pl.ds(count * rows, EXTRA), :] = total.astype(out.dtype)


def products(operands, table, plan, kinds, cross=None, cross_made=False, terms=(), weight=1):
    shapes = []
    for (_, count, _, rows, ring, _), kind in zip(plan, kinds):
        shape = (count * rows + EXTRA, BLK) if ring else (count, rows, BLK)
        shapes.append(jax.ShapeDtypeStruct(shape, kind))
    if cross_made:
        shapes.append(jax.ShapeDtypeStruct((EXTRA, BLK), F32))
    vmem = pl.BlockSpec(memory_space=pltpu.VMEM)
    opening = len(operands) == 6
    if opening:
        half, deep = operands[0].shape
        shapes += [jax.ShapeDtypeStruct((2 * half, 2 * deep), BF), jax.ShapeDtypeStruct((2 * deep, 2 * half), BF)]
    extra = () if cross is None else (cross,)
    return pl.pallas_call(
        functools.partial(product_kernel, plan, opening, cross_made, cross is not None),
        out_shape=shapes,
        in_specs=[pl.BlockSpec(memory_space=pltpu.SMEM)] + [vmem] * (len(operands) + len(extra) + len(terms)),
        out_specs=[vmem] * len(shapes),
        scratch_shapes=[pltpu.SemaphoreType.DMA((6,))] if opening else [],
        compiler_params=grant(24),
        cost_estimate=cost(weight),
    )(table, *operands, *extra, *terms)


def call_sum(kernel, shapes, *operands):
    vmem = pl.BlockSpec(memory_space=pltpu.VMEM)
    return pl.pallas_call(
        kernel,
        out_shape=[jax.ShapeDtypeStruct(shape, kind) for shape, kind in shapes],
        in_specs=[vmem] * len(operands),
        out_specs=[vmem] * len(shapes),
        compiler_params=grant(12),
        cost_estimate=cost(1),
    )(*operands)


def add_kernel(own, got, out):
    out[...] = (own[...] + got[...].astype(F32)).astype(out.dtype)


def home_kernel(*refs):
    homes, (got_3p, got_2m, got_2p, got_3m), outs = refs[:4], refs[4:8], refs[8:]
    for d, (home, out) in enumerate(zip(homes, outs)):
        one, two = (got_3p, got_2m) if d < 2 else (got_2p, got_3m)
        half = pl.ds(4 * (d % 2), 4)
        out[...] = (home[...] + one[half].astype(F32) + two[half].astype(F32)).astype(out.dtype)


def home_rest_kernel(*refs):
    homes, got, outs = refs[:4], refs[4], refs[5:]
    quarter = homes[0].shape[0] - EXTRA
    for d, (home, out) in enumerate(zip(homes, outs)):
        out[pl.ds(0, quarter), :] = (
            home[pl.ds(0, quarter), :] + got[pl.ds(d * quarter, quarter), :].astype(F32)
        ).astype(out.dtype)
        out[pl.ds(quarter, EXTRA), :] = (
            home[pl.ds(quarter, EXTRA), :] + got[pl.ds(4 * quarter, EXTRA), :].astype(F32)
        ).astype(out.dtype)


def main_sum_kernel(own, second, first, third, *outs):
    for d, out in enumerate(outs):
        total = own[d]
        for ref in (second, first, third):
            total = total + ref[d].astype(F32)
        out[...] = total


def rest_sum_kernel(own, second, first, third, *outs):
    quarter = own.shape[0] - EXTRA
    cross = own[pl.ds(quarter, EXTRA), :][0:1]
    for d, ref in ((2, second), (1, first), (3, third)):
        cross = cross + ref[pl.ds(quarter, EXTRA), :].astype(F32)[d : d + 1]
    cross = jnp.broadcast_to(cross, (8, BLK))
    for d, out in enumerate(outs):
        part = pl.ds(d * REST, REST)
        total = own[part, :]
        for ref in (second, first, third):
            total = total + ref[part, :].astype(F32)
        out[pl.ds(0, REST), :] = total
        out[pl.ds(REST, 8), :] = cross


def last_sum_kernel(*refs):
    mains, rests, (out, sent) = refs[:4], refs[4:8], refs[8:]
    main = mains[0][...] + mains[1][...] + mains[2][...] + mains[3][...]
    rest = rests[0][...] + rests[1][...] + rests[2][...] + rests[3][...]
    out[pl.ds(0, MAIN), :] = main
    out[pl.ds(MAIN, REST + 8), :] = rest
    sent[pl.ds(0, MAIN), :] = main.astype(sent.dtype)
    sent[pl.ds(MAIN, REST), :] = rest[:REST].astype(sent.dtype)


def finish_kernel(state, scale, here_ref, got_ref, out_ref):
    s, fold = state[0], state[1]
    here = here_ref[pl.ds(0, BLK), :] * scale
    got = got_ref[...].T.astype(F32) * scale
    first_at, second_at = pl.multiple_of(s * BLK, BLK), pl.multiple_of((1 - s) * BLK, BLK)

    @pl.when(fold == 0)
    def _():
        out_ref[:, pl.ds(first_at, BLK)] = here
        out_ref[:, pl.ds(second_at, BLK)] = got

    @pl.when(fold == 1)
    def _():
        i = lax.broadcasted_iota(jnp.int32, (BLK, BLK), 0)
        j = lax.broadcasted_iota(jnp.int32, (BLK, BLK), 1)
        cross = here_ref[pl.ds(BLK, 8), :][0:1] * scale
        out_ref[:, pl.ds(first_at, BLK)] = jnp.where(i >= j, here, here.T)
        out_ref[:, pl.ds(second_at, BLK)] = jnp.where(i == j, cross, jnp.where(i > j, got, here))


def local(design, weight, counts, column_map):
    rows_here = design.shape[0]
    core = lax.axis_index("core")
    place = {name: lax.axis_index(name) for name in ("z", "y", "x")}
    total_rows = rows_here * 128

    own_low, own_high = scaled_rows(column_map, counts, weight, design)

    def move(array, pairs):
        return lax.ppermute(array, AXES, pairs)

    M, R = MAIN_ORDER, REST_ORDER

    def main_to(stage, step):
        return shift_pairs(*M, stage, step)

    def rest_to(stage, step):
        return shift_pairs(*R, stage, step)

    swap = [(0, 1), (1, 0)]
    other_low = lax.ppermute(own_low, "core", swap)
    other_high = lax.ppermute(own_high, "core", swap)
    half = own_low.shape
    own_turned, low_turned = pl.pallas_call(
        turn_kernel,
        out_shape=[
            jax.ShapeDtypeStruct((half[1], 2 * half[0]), BF),
            jax.ShapeDtypeStruct((half[1], half[0]), BF),
        ],
        in_specs=[pl.BlockSpec(memory_space=pltpu.VMEM)] * 3,
        out_specs=[pl.BlockSpec(memory_space=pltpu.VMEM)] * 2,
        compiler_params=grant(12),
        cost_estimate=cost(1),
    )(own_low, own_high, other_low)

    plus = [(a, b) for a in (0, 1) for b in range(4)]
    minus = [(a, b) for a in (2, 3) for b in range(4)]
    every = plus + minus
    tables = [cross_table()]

    def blocks(order, d, rest, *added):
        first = sum(t.shape[1] for t in tables) // 4
        tables.append(block_table(order, [(d,) + p for p in rest]))
        row0, rows = (0, MAIN) if order is M else (MAIN, REST)
        return first, len(rest), row0, rows, order is R, added

    plan_1 = [blocks(M, 2, plus), blocks(M, 2, minus)]
    plan_1r = [blocks(R, 3, every)]
    plan_2 = [blocks(M, 1, minus), blocks(M, 3, plus)]
    plan_2r = [blocks(R, 2, every, (0, 0))]
    plan_3 = [blocks(M, 1, plus, (0, 0)), blocks(M, 3, minus, (1, 0))]
    plan_3r = [blocks(R, 1, every)]
    plan_4 = [
        blocks(M, 0, every[4 * d : 4 * d + 4])
        for d in range(4)
    ]
    plan_4r = [blocks(R, 0, every[4 * d : 4 * d + 4]) for d in range(4)]
    device = ((place["z"] * 4 + place["y"]) * 4 + place["x"]) * 2 + core
    table = lax.dynamic_index_in_dim(
        jnp.asarray(np.concatenate(tables, axis=1)), device, 0, keepdims=False
    )

    pieces = (own_low, own_high, other_low, other_high, own_turned, low_turned)
    ring, cross, *both = products(pieces, table, plan_1r, (BF,), cross_made=True)
    got_r = move(ring, rest_to(0, 1))
    first_p, first_m = products(both, table, plan_1, (BF, BF))
    got_1p = move(first_p, main_to(0, 1))
    got_1m = move(first_m, main_to(0, -1))
    both, first_p = lax.optimization_barrier((both, first_p))
    side_p, side_m = products(both, table, plan_2, (BF, BF))
    got_2p = move(side_p, main_to(0, 1))
    got_2m = move(side_m, main_to(0, -1))
    both, side_p = lax.optimization_barrier((both, side_p))
    (ring,) = products(both, table, plan_2r, (BF,), cross, terms=(got_r,))
    got_r = move(ring, rest_to(0, 1))
    both, ring = lax.optimization_barrier((both, ring))
    relay_p, relay_m = products(both, table, plan_3, (BF, BF), terms=(got_1p, got_1m))
    got_3p = move(relay_p, main_to(0, 1))
    got_3m = move(relay_m, main_to(0, -1))
    both, relay_p, got_2p, got_2m = lax.optimization_barrier((both, relay_p, got_2p, got_2m))
    (line,) = products(both, table, plan_3r, (F32,), cross, weight=WEIGHT)
    (ring,) = call_sum(add_kernel, [(line.shape, BF)], line, got_r)
    got_r = move(ring, rest_to(0, 1))
    both, ring = lax.optimization_barrier((both, ring))
    home = products(both, table, plan_4, (F32,) * 4, weight=WEIGHT)
    both, home = lax.optimization_barrier((both, home))
    line = products(both, table, plan_4r, (F32,) * 4, cross, weight=WEIGHT)
    part = call_sum(
        home_kernel, [(h.shape, F32 if d == 0 else BF) for d, h in enumerate(home)], *home, got_3p, got_2m, got_2p, got_3m
    )
    rest = call_sum(home_rest_kernel, [(h.shape, F32 if d == 0 else BF) for d, h in enumerate(line)], *line, got_r)

    got = [move(part[d], main_to(1, d)) for d in (2, 1, 3)]
    got_r = [move(rest[d], rest_to(1, d)) for d in (2, 1, 3)]
    got, got_r = lax.optimization_barrier((got, got_r))
    part = call_sum(main_sum_kernel, [((MAIN, BLK), F32)] * 4, part[0], *got)
    part, got_r = lax.optimization_barrier((part, got_r))
    rest = call_sum(rest_sum_kernel, [((REST + 8, BLK), F32)] * 4, rest[0], *got_r)

    got = [move(part[d], main_to(2, d)) for d in (2, 1, 3)]
    got_r = [move(rest[d], rest_to(2, d)) for d in (2, 1, 3)]
    here, sent = call_sum(
        last_sum_kernel, [((BLK + 8, BLK), F32), ((BLK, BLK), F32)], part[0], *got, rest[0], *got_r
    )
    got = move(sent, mirror_pairs())

    r, c = 4 * place["z"] + place["y"], 2 * place["x"] + core
    i, h = r // 2, r % 2
    s = jnp.where(i <= c, h, 1 - h)
    state = jnp.stack([s, (i == c).astype(jnp.int32)]).astype(jnp.int32)
    vmem = pl.BlockSpec(memory_space=pltpu.VMEM)
    return pl.pallas_call(
        lambda *refs: finish_kernel(refs[0], 1.0 / total_rows, *refs[1:]),
        out_shape=jax.ShapeDtypeStruct((BLK, 2 * BLK), F32),
        in_specs=[pl.BlockSpec(memory_space=pltpu.SMEM)] + [vmem] * 2,
        out_specs=vmem,
        compiler_params=pltpu.CompilerParams(vmem_limit_bytes=16 * 1024 * 1024),
    )(state, here, got)


def solution(mesh):
    fine = Mesh(mesh.devices.reshape(4, 4, 4, 2), AXES)
    return jax.shard_map(
        local,
        mesh=fine,
        in_specs=(P(AXES, None), P(AXES), P(AXES), P()),
        out_specs=P(("z", "y"), ("x", "core")),
        check_vma=False,
    )
```
